128 devices in a mesh: sample: 4 (over z_hi, core), row: 32 (over x, z_lo, y).
Axes of the slice: x: 4, y: 4, z: 4 (z_hi: 2, z_lo: 2; z = z_hi * 2 + z_lo), core: 2. Of those that a mesh axis runs over, the one named last changes fastest.
Arguments:
- fine_state: float32 [8, 512, 16384], P('sample', 'row'), parts along dimension 0, may hold values from -3 to 3
- noise: bfloat16 [12, 2, 512, 16384], P('sample', None, 'row'), parts along dimension 0, may hold values from -6 to 6
Outputs:
- fine_final: float32 [8, 512, 16384], P('sample', 'row'), parts along dimension 0
- coarse_final: float32 [8, 128, 4096], P('sample', 'row'), parts along dimension 0
- correction: float32 [8, 512, 16384], P('sample', 'row'), parts along dimension 0
The draws below stay inside these ranges and needn't reach their ends.
There are 4 independent parts, one for each index of `sample`. The reference program is written for one: setup_inputs(seed, part) draws one part's arguments, and reference() takes and returns one part's arrays. A program takes and returns all parts, laid end to end along the dimension named above; each array names one. Nothing has to cross between parts.
All inputs are finite; a program needn't handle non-finite values.
Results may differ from the reference program's by a relative error of at most 0.0003.
Values sent between devices are 32-bit elements; how exact they have to be, the bound alone decides.
No kernel may reach another device: no remote copies, remote signals or barrier semaphores. Data moves between devices by JAX's collectives and lax.ppermute only.
A program may use at most 192 MiB of HBM per device.

```python
import math
import jax
import jax.numpy as jnp

NF = 16384
NFR = 512


def wave_field(key, amplitude, mode_count):
    row_ids = jnp.arange(NFR, dtype=jnp.int32)[:, None]
    col_ids = jnp.arange(NF, dtype=jnp.int32)[None, :]
    row_top = max(2, NFR // 64 + 1)
    col_top = max(2, NF // 64 + 1)
    summed_waves = jnp.zeros((NFR, NF), jnp.float32)
    for index_mode in range(mode_count):
        mode_key = jax.random.fold_in(key, index_mode)
        mode_keys = jax.random.split(mode_key, 4)
        row_freq = jax.random.randint(mode_keys[0], (), 1, row_top).astype(jnp.int32)
        col_freq = jax.random.randint(mode_keys[1], (), 1, col_top).astype(jnp.int32)
        phase_shift = jax.random.uniform(mode_keys[2], (), jnp.float32, 0.0, 2.0 * math.pi)
        mode_weight = jax.random.uniform(mode_keys[3], (), jnp.float32, 0.5, 1.5)
        row_frac = (row_ids * row_freq % NFR).astype(jnp.float32) / NFR
        col_frac = (col_ids * col_freq % NF).astype(jnp.float32) / NF
        summed_waves = summed_waves + mode_weight * jnp.sin(2.0 * math.pi * (row_frac + col_frac) + phase_shift)
    return summed_waves * (amplitude / math.sqrt(mode_count / 2.0))


def draw_fine_state(key, part):
    key = jax.random.fold_in(key, 11)
    subkeys = jax.random.split(key, 4)
    activator = -0.5 + wave_field(subkeys[0], 1.0, 6) + 0.35 * jax.random.normal(subkeys[2], (NFR, NF), jnp.float32)
    inhibitor = -0.25 + wave_field(subkeys[1], 0.6, 6) + 0.25 * jax.random.normal(subkeys[3], (NFR, NF), jnp.float32)
    stacked = jnp.stack([activator, inhibitor])
    return 2.95 * jnp.tanh(stacked / 2.95)


def levels(own_key, dims, shards, least, largest):
    level, own = 1.0, jax.random.fold_in(own_key, 6)
    for position, shards_of in shards:
        steps = jnp.exp(jax.random.uniform(jax.random.fold_in(own, position), (shards_of,), jnp.float32, least / len(shards), largest / len(shards)))
        level = level * jnp.repeat(steps, dims[position] // shards_of).reshape([-1 if axis == position else 1 for axis in range(len(dims))])
    return level


def bell_draw(own_key, dims, width, reach, cuts=(), kind=jnp.bfloat16):
    gain = levels(own_key, dims, cuts, -0.22, 0.18) if cuts else 1.0
    array = jax.random.normal(own_key, dims, jnp.float32) * width * gain
    return jnp.minimum(jnp.maximum(array, -reach), reach).astype(kind)


def setup_inputs(seed: int = 0, part: int = 0) -> dict:
    key_list = jax.random.split(jax.random.key(seed), 3)
    part_splits = jax.random.split(jax.random.fold_in(key_list[2], part), 3)
    return {
        "fine_state": draw_fine_state(jax.random.fold_in(jax.random.fold_in(key_list[2], part), 71), part),
        "noise": bell_draw(part_splits[1], (3, 2, NFR, NF), 1.0, 6.0, ((2, 32),)),
    }


def laplace_rows(extended):
    total_rows = extended.shape[1]
    padded = jnp.pad(extended, ((0, 0), (0, 0), (2, 2)))
    middle = padded[:, 2:total_rows - 2, 2:-2]
    nearby = padded[:, 1:total_rows - 3, 2:-2] + padded[:, 3:total_rows - 1, 2:-2]
    nearby = nearby + padded[:, 2:total_rows - 2, 1:-3] + padded[:, 2:total_rows - 2, 3:-1]
    distant = padded[:, 0:total_rows - 4, 2:-2] + padded[:, 4:total_rows, 2:-2]
    distant = distant + padded[:, 2:total_rows - 2, 0:-4] + padded[:, 2:total_rows - 2, 4:]
    return (4.0 / 3.0) * nearby - distant / 12.0 - 5.0 * middle


def update(center, laplace, forcing, diffuse_scale, reaction_step, noise_gain):
    activator = center[0]
    inhibitor = center[1]
    new_activator = activator + 0.15 * diffuse_scale * laplace[0] + reaction_step * (activator - activator * activator * activator / 3.0 - inhibitor) + noise_gain * forcing[0]
    new_inhibitor = inhibitor + 0.05 * diffuse_scale * laplace[1] + reaction_step * 0.08 * (activator + 0.7 - 0.8 * inhibitor) + noise_gain * forcing[1]
    return jnp.stack([new_activator, new_inhibitor])


def restrict(field_data):
    count, rows_all, cols_all = field_data.shape
    return field_data.reshape(count, rows_all // 4, 4, cols_all // 4, 4).mean(axis=(2, 4))


def reference(fine_state, noise):
    field_now = fine_state
    for step in range(3):
        extended = jnp.pad(field_now, ((0, 0), (2, 2), (0, 0)))
        field_now = update(field_now, laplace_rows(extended), noise[step].astype(jnp.float32), 1.0, 0.05, 0.25)
    coarse_start = restrict(fine_state)
    summed = noise[0].astype(jnp.float32) + noise[1].astype(jnp.float32) + noise[2].astype(jnp.float32)
    coarse_noise = restrict(summed)
    extended = jnp.pad(coarse_start, ((0, 0), (2, 2), (0, 0)))
    coarse_final = update(coarse_start, laplace_rows(extended), coarse_noise, 3.0 / 16.0, 0.15, 1.0)
    prolonged = jnp.repeat(jnp.repeat(coarse_final, 4, axis=1), 4, axis=2)
    return field_now, coarse_final, field_now - prolonged
```

```python
import functools

import jax
import jax.numpy as jnp
from jax import lax
from jax.experimental import pallas as pl
from jax.experimental.pallas import tpu as pltpu
from jax.sharding import PartitionSpec as P

NEAR, FAR = 4.0 / 3.0, -1.0 / 12.0
DIFFUSE = (0.15, 0.05)
MIB = 1 << 20


def iota(dim):
    return lax.broadcasted_iota(jnp.int32, (8, 128), dim)


def pick(x, index):
    return jnp.take_along_axis(x, index, axis=0, mode="promise_in_bounds")


def turn(x, steps):
    return pltpu.roll(x, steps, 0)


def sideways(mid, left, right, lane):
    near = pltpu.roll(jnp.where(lane == 127, left, mid), 1, 1) + pltpu.roll(
        jnp.where(lane == 0, right, mid), 127, 1
    )
    far = pltpu.roll(jnp.where(lane >= 126, left, mid), 2, 1) + pltpu.roll(
        jnp.where(lane < 2, right, mid), 126, 1
    )
    return near, far


def stepped(a, b, near, far, force, scale, react):
    da, db = DIFFUSE[0] * scale, DIFFUSE[1] * scale
    new_a = a * ((1.0 + react - 5.0 * da) - (react / 3.0) * (a * a)) - react * b
    new_a = new_a + (da * NEAR) * near[0] + (da * FAR) * far[0] + force[0]
    low = 0.08 * react
    new_b = b * (1.0 - 5.0 * db - 0.8 * low) + low * a + 0.7 * low
    new_b = new_b + (db * NEAR) * near[1] + (db * FAR) * far[1] + force[1]
    return new_a, new_b


def both_ends(ref, which, first, sub):
    block = which.astype(jnp.float32)
    half = sub >> 1
    top = pick(block[0:8], half + first)
    low = pick(block[8:16], 7 - first - half)
    return jnp.where((sub & 1) == 0, top, low)


def pre_kernel(row_axis, f_hbm, n_hbm, m_odd, m_even, x0, f1, own, own_q, fbuf, nbuf, sems):
    nb = x0.shape[1] - 2
    chunks = 4
    width = nb // chunks
    copies = []
    for c in range(chunks):
        cols = pl.ds(c * width * 128, width * 128)
        copies.append(
            (
                pltpu.make_async_copy(f_hbm.at[:, :, cols], fbuf.at[:, :, cols], sems.at[0, c]),
                pltpu.make_async_copy(
                    n_hbm.at[0:2, :, :, cols], nbuf.at[:, :, :, cols], sems.at[1, c]
                ),
            )
        )
        copies[-1][0].start()
        copies[-1][1].start()
    sub, lane = iota(0), iota(1)
    parity = lax.rem(lax.axis_index(row_axis), 2)
    zero = jnp.zeros((8, 128), jnp.float32)
    for f in range(2):
        for edge in (0, nb + 1):
            for r in range(3):
                x0[f, edge, 8 * r : 8 * r + 8] = zero
            f1[f, edge] = zero

    def fill(j):
        cols = pl.ds(pl.multiple_of(j * 128, 128), 128)
        for f in range(2):
            x0[f, j + 1, 0:4] = zero[0:4]
            x0[f, j + 1, pl.ds(4, 8, stride=2)] = fbuf[f, 0:8, cols]
            x0[f, j + 1, pl.ds(5, 8, stride=2)] = pick(fbuf[f, 8:16, cols], 7 - sub)

    def edge_step(j):
        cols = pl.ds(pl.multiple_of(j * 128, 128), 128)
        jj = j + 1
        mids, nears, fars, forces, rims = [], [], [], [], []
        for f in range(2):
            mid = x0[f, jj, 4:12]
            up1, up2 = x0[f, jj, 2:10], x0[f, jj, 0:8]
            near, far = sideways(mid, x0[f, jj - 1, 4:12], x0[f, jj + 1, 4:12], lane)
            nears.append(near + (up1 + x0[f, jj, 6:14]))
            fars.append(far + (up2 + x0[f, jj, 8:16]))
            forces.append(0.25 * both_ends(None, nbuf[0, f, :, cols], 0, sub))
            mids.append(mid)
            rims.append((DIFFUSE[f] * NEAR) * up1 + (DIFFUSE[f] * FAR) * mid)
        new = stepped(mids[0], mids[1], nears, fars, forces, 1.0, 0.05)
        wins, qs = [], []
        for f in range(2):
            half = turn(new[f], 4)
            f1[f, jj] = new[f]
            win = jnp.where(sub < 4, rims[f], half)
            own[f, j] = win
            q = 0.25 * both_ends(None, nbuf[1, f, :, cols], 0, sub)
            q = q + (DIFFUSE[f] * FAR) * half
            q = q + jnp.where(sub >= 2, (DIFFUSE[f] * NEAR) * turn(new[f], 6), 0.0)
            own_q[f, j] = turn(q, 4)
            wins.append(win)
            qs.append(q)
        return wins, qs

    def pair(i):
        wins0, qs0 = edge_step(2 * i)
        wins1, qs1 = edge_step(2 * i + 1)
        for out, side in ((m_odd, parity), (m_even, 1 - parity)):
            at = 6 - 2 * (sub & 3) + side
            out[2 * i] = jnp.where(sub < 4, pick(wins0[0], at), pick(wins0[1], at))
            out[2 * i + 1] = jnp.where(sub < 4, pick(wins1[0], at), pick(wins1[1], at))
            at = 2 - 2 * (sub & 1) + side
            first = jnp.where((sub & 2) == 0, pick(qs0[0], at), pick(qs0[1], at))
            second = jnp.where((sub & 2) == 0, pick(qs1[0], at), pick(qs1[1], at))
            out[nb + i] = jnp.where(sub < 4, first, second)

    def loop(lo, hi, body, unroll):
        if hi > lo:
            lax.fori_loop(lo, hi, lambda i, c: (body(i), c)[1], 0, unroll=unroll)

    done = 0
    for c in range(chunks):
        copies[c][0].wait()
        loop(c * width, (c + 1) * width, fill, 4)
        copies[c][1].wait()
        ready = nb if c == chunks - 1 else (c + 1) * width - 2
        loop(done // 2, ready // 2, pair, 2)
        done = ready


def averaging(k, value, transpose):
    row = lax.broadcasted_iota(jnp.int32, (128, 128), 0)
    col = lax.broadcasted_iota(jnp.int32, (128, 128), 1)
    fine, coarse = (col, row) if transpose else (row, col)
    return jnp.where(coarse == 32 * k + (fine >> 2), jnp.float32(value), jnp.float32(0.0))


def lanes_averaged(held):
    groups = held.shape[1]
    total = jnp.zeros((groups * 8, 128), jnp.float32)
    for k in range(4):
        total = total + jnp.dot(
            held[k].reshape(groups * 8, 128),
            averaging(k, 1.0 / 16.0, False),
            preferred_element_type=jnp.float32,
            precision=lax.Precision.HIGHEST,
        )
    return total.reshape(groups, 8, 128)


def coarse_start_kernel(row_axis, x0, start, m_odd, m_even, held):
    nb = x0.shape[1] - 2
    groups = nb // 4
    sub = iota(0)
    parity = lax.rem(lax.axis_index(row_axis), 2)

    def group(g, carry):
        for k in range(4):
            sums = []
            for f in range(2):
                parts = []
                for r in (4, 12):
                    x = x0[f, 4 * g + k + 1, r : r + 8]
                    x = x + turn(x, 4)
                    parts.append(x + turn(x, 2))
                sums.append(jnp.where((sub & 3) < 2, parts[0], parts[1]))
            held[k, g] = jnp.where(sub < 4, sums[0], sums[1])
        return carry

    lax.fori_loop(0, groups, group, 0)
    zero = jnp.zeros((8, 128), jnp.float32)
    start[0] = zero
    start[groups + 1] = zero
    start[1 : groups + 1] = lanes_averaged(held)

    def message(i, carry):
        rims = []
        for h in range(2):
            c = start[2 * i + h + 1]
            rims.append(jnp.where((sub & 2) == 0, NEAR * c, 0.0) + FAR * pick(c, sub ^ 2))
        for out, side in ((m_odd, parity), (m_even, 1 - parity)):
            at = 4 * ((sub >> 1) & 1) + 2 * (sub & 1) + side
            out[i] = jnp.where(sub < 4, pick(rims[0], at), pick(rims[1], at))
        return carry

    lax.fori_loop(0, groups // 2, message, 0)


def inner_kernel(x0, f1, noise, p2, p3, n2, g1, g2):
    nb = x0.shape[1] - 2
    sub, lane = iota(0), iota(1)
    zero = jnp.zeros((8, 128), jnp.float32)
    for f in range(2):
        for edge in (0, nb + 1):
            g1[f, edge] = zero
            g2[f, edge] = zero
    half = sub >> 1
    down1 = jnp.where(sub < 6, sub + 2, 13 - sub)
    down2 = jnp.where(sub < 4, sub + 4, 11 - sub)

    def first(j, carry):
        cols = pl.ds(pl.multiple_of(j * 128, 128), 128)
        jj = j + 1
        mids, nears, fars, forces = [], [], [], []
        for f in range(2):
            mid = x0[f, jj, 12:20]
            near, far = sideways(mid, x0[f, jj - 1, 12:20], x0[f, jj + 1, 12:20], lane)
            nears.append(near + (x0[f, jj, 10:18] + pick(mid, down1)))
            fars.append(far + (x0[f, jj, 8:16] + pick(mid, down2)))
            forces.append(0.25 * both_ends(None, noise[0, f, :, cols], 4, sub))
            mids.append(mid)
        new = stepped(mids[0], mids[1], nears, fars, forces, 1.0, 0.05)
        for f in range(2):
            g1[f, jj] = new[f]
        return carry

    def second(j, carry):
        cols = pl.ds(pl.multiple_of(j * 128, 128), 128)
        jj = j + 1
        mids, nears, fars, forces = [], [], [], []
        tops, top_nears, top_fars, top_forces = [], [], [], []
        for f in range(2):
            mid, top = g1[f, jj], f1[f, jj]
            near, far = sideways(mid, g1[f, jj - 1], g1[f, jj + 1], lane)
            up1 = jnp.where(sub < 2, turn(top, 2), turn(mid, 2))
            up2 = jnp.where(sub < 4, turn(top, 4), turn(mid, 4))
            nears.append(near + (up1 + pick(mid, down1)))
            fars.append(far + (up2 + pick(mid, down2)))
            forces.append(0.25 * both_ends(None, noise[1, f, :, cols], 4, sub))
            mids.append(mid)
            near, far = sideways(top, f1[f, jj - 1], f1[f, jj + 1], lane)
            up1 = jnp.where(sub < 6, 0.0, turn(top, 2))
            low1 = jnp.where(sub < 6, turn(top, 6), turn(mid, 6))
            low2 = jnp.where(sub < 4, turn(top, 4), turn(mid, 4))
            top_nears.append(near + (up1 + low1))
            top_fars.append(far + low2)
            top_forces.append(0.25 * both_ends(None, noise[1, f, :, cols], 0, sub))
            tops.append(top)
        new = stepped(mids[0], mids[1], nears, fars, forces, 1.0, 0.05)
        part = stepped(tops[0], tops[1], top_nears, top_fars, top_forces, 1.0, 0.05)
        for f in range(2):
            g2[f, jj] = new[f]
            p2[f, j] = jnp.where(sub < 4, turn(part[f], 4), turn(new[f], 4))
        return carry

    def third(j, carry):
        cols = pl.ds(pl.multiple_of(j * 128, 128), 128)
        jj = j + 1
        mids, nears, fars, forces = [], [], [], []
        for f in range(2):
            mid = g2[f, jj]
            near, far = sideways(mid, g2[f, jj - 1], g2[f, jj + 1], lane)
            up1 = jnp.where(sub < 2, 0.0, turn(mid, 2))
            up2 = jnp.where(sub < 4, 0.0, turn(mid, 4))
            nears.append(near + (up1 + pick(mid, down1)))
            fars.append(far + (up2 + pick(mid, down2)))
            forces.append(0.25 * both_ends(None, noise[2, f, :, cols], 4, sub))
            n2[f, j] = 0.25 * both_ends(None, noise[2, f, :, cols], 0, sub)
            mids.append(mid)
        new = stepped(mids[0], mids[1], nears, fars, forces, 1.0, 0.05)
        for f in range(2):
            p3[f, j] = new[f]
        return carry

    lax.fori_loop(0, nb, first, 0, unroll=2)
    lax.fori_loop(0, nb, second, 0)
    lax.fori_loop(0, nb, third, 0, unroll=2)


def coarse_kernel(row_axis, start, noise, m_odd, m_even, coarse, spread, held, push):
    groups = start.shape[0] - 2
    sub, lane = iota(0), iota(1)
    parity = lax.rem(lax.axis_index(row_axis), 2)
    mine = (sub & 1) == parity

    def gather_noise(g, carry):
        for k in range(4):
            cols = pl.ds(pl.multiple_of((4 * g + k) * 128, 128), 128)
            sums = []
            for f in range(2):
                total = noise[0, f, :, cols].astype(jnp.float32)
                total = total + noise[1, f, :, cols].astype(jnp.float32)
                total = total + noise[2, f, :, cols].astype(jnp.float32)
                parts = []
                for r in (0, 8):
                    x = total[r : r + 8]
                    x = x + turn(x, 7)
                    parts.append(x + turn(x, 6))
                sums.append(
                    jnp.where(
                        (sub & 1) == 0,
                        pick(parts[0], (sub & 2) * 2),
                        pick(parts[1], 4 - (sub & 2) * 2),
                    )
                )
            held[k, g] = jnp.where(sub < 4, sums[0], sums[1])
        return carry

    lax.fori_loop(0, groups, gather_noise, 0)
    push[...] = lanes_averaged(held)

    is_a = sub < 4
    scale, react = 3.0 / 16.0, 0.15
    diffuse = jnp.where(is_a, DIFFUSE[0] * scale, DIFFUSE[1] * scale)
    order = jnp.where(sub < 1, 0, jnp.where(sub < 2, 2, jnp.where(sub < 3, 3, 1)))

    def update(g, carry):
        pairs = g // 2
        base = 4 * (g - 2 * pairs)
        c = start[g + 1]
        near, far = sideways(c, start[g], start[g + 2], lane)
        inward = jnp.where((sub & 2) == 0, sub + 2, sub ^ 1)
        near = near + pick(c, inward) + jnp.where((sub & 2) == 0, 0.0, turn(c, 2))
        far = far + pick(c, (sub & 4) + 3 - (sub & 3))
        at = base + (sub >> 1)
        rim = jnp.where(mine, pick(m_odd[pairs], at), pick(m_even[pairs], at))
        lap = NEAR * near + FAR * far + rim - 5.0 * c
        other = turn(c, 4)
        change = jnp.where(
            is_a, react * (c - c * c * c / 3.0 - other), (react * 0.08) * (other + 0.7 - 0.8 * c)
        )
        new = c + diffuse * lap + change + push[g]
        push[g] = new
        cols = pl.ds(pl.multiple_of(g * 128, 128), 128)
        for f in range(2):
            coarse[f, :, cols] = pick(new, order + 4 * f)[0:4]
        return carry

    lax.fori_loop(0, groups, update, 0)
    for k in range(4):
        held[k] = jnp.dot(
            push[...].reshape(groups * 8, 128),
            averaging(k, 1.0, True),
            preferred_element_type=jnp.float32,
            precision=lax.Precision.HIGHEST,
        ).reshape(groups, 8, 128)

    def spread_rows(g, carry):
        for k in range(4):
            x = held[k, g]
            for f in range(2):
                spread[4 * g + k, 2 * f] = pick(x, 4 * f + jnp.where(sub < 4, 0, 2))
                spread[4 * g + k, 2 * f + 1] = pick(x, 4 * f + jnp.where(sub < 4, 3, 1))
        return carry

    lax.fori_loop(0, groups, spread_rows, 0)


def post_kernel(
    row_axis, m_odd, m_even, own, own_q, p2, p3, n2, spread, fine, corr, g1, g2, fbuf, cbuf, sems
):
    nb = own.shape[1]
    chunks = 4
    width = nb // chunks
    sub, lane = iota(0), iota(1)
    place = lax.axis_index(row_axis)
    parity = lax.rem(place, 2)
    last = lax.axis_size(row_axis) - 1
    mine = (sub & 1) == parity
    outside = ((place == 0) & ((sub & 1) == 0)) | ((place == last) & ((sub & 1) == 1))
    keep = jnp.where(outside & (sub < 4), jnp.float32(0.0), jnp.float32(1.0))
    half = sub >> 1
    zero = jnp.zeros((8, 128), jnp.float32)
    for f in range(2):
        for edge in (0, nb + 1):
            for r in range(3):
                g1[f, edge, 8 * r : 8 * r + 8] = zero
            for r in range(2):
                g2[f, edge, 8 * r : 8 * r + 8] = zero
    close = [jnp.where(sub < 2, DIFFUSE[f] * NEAR, 0.0) for f in range(2)]
    wide = [jnp.where(sub < 4, DIFFUSE[f] * FAR, 0.0) for f in range(2)]
    even_rows = (2 * sub) & 7

    def first(j):
        odd, even = m_odd[j], m_even[j]
        for f in range(2):
            came = jnp.where(mine, pick(odd, half + 4 * f), pick(even, half + 4 * f))
            g1[f, j + 1, 0:8] = zero
            g1[f, j + 1, 8:16] = (came + own[f, j]) * keep
            g1[f, j + 1, 16:24] = zero

    def second_at(j, odd, even, base):
        jj = j + 1
        mids, nears, fars, forces, twos = [], [], [], [], []
        for f in range(2):
            mid = g1[f, jj, 8:16]
            low2 = g1[f, jj, 12:20]
            near, far = sideways(mid, g1[f, jj - 1, 8:16], g1[f, jj + 1, 8:16], lane)
            nears.append(near + (g1[f, jj, 6:14] + g1[f, jj, 10:18]))
            fars.append(far + (g1[f, jj, 4:12] + low2))
            at = (half & 1) + (2 * f + base)
            came = jnp.where(mine, pick(odd, at), pick(even, at))
            forces.append(jnp.where(sub < 4, came, own_q[f, j]))
            mids.append(mid)
            more = (DIFFUSE[f] * NEAR) * g1[f, jj, 14:22] + (DIFFUSE[f] * FAR) * low2
            g2[f, jj, 8:16] = p2[f, j] + more
        new = stepped(mids[0], mids[1], nears, fars, forces, 1.0, 0.05)
        for f in range(2):
            g2[f, jj, 0:8] = new[f] * keep

    def second(i):
        odd, even = m_odd[nb + i], m_even[nb + i]
        second_at(2 * i, odd, even, 0)
        second_at(2 * i + 1, odd, even, 4)

    def third(j):
        cols = pl.ds(pl.multiple_of(j * 128, 128), 128)
        jj = j + 1
        mids, nears, fars, forces, lows = [], [], [], [], []
        for f in range(2):
            mid = g2[f, jj, 4:12]
            low2 = g2[f, jj, 8:16]
            near, far = sideways(mid, g2[f, jj - 1, 4:12], g2[f, jj + 1, 4:12], lane)
            nears.append(near + (g2[f, jj, 2:10] + g2[f, jj, 6:14]))
            fars.append(far + (g2[f, jj, 0:8] + low2))
            forces.append(n2[f, j])
            mids.append(mid)
            lows.append(p3[f, j] + close[f] * turn(low2, 6) + wide[f] * low2)
        new = stepped(mids[0], mids[1], nears, fars, forces, 1.0, 0.05)
        for f in range(2):
            top = jnp.where(sub < 4, pick(new[f], even_rows), pick(lows[f], even_rows))
            low = jnp.where(sub < 4, pick(lows[f], 7 - even_rows), pick(new[f], 7 - even_rows))
            fbuf[f, 0:8, cols] = top
            fbuf[f, 8:16, cols] = low
            cbuf[f, 0:8, cols] = top - spread[j, 2 * f]
            cbuf[f, 8:16, cols] = low - spread[j, 2 * f + 1]

    def loop(lo, hi, body, unroll):
        if hi > lo:
            lax.fori_loop(lo, hi, lambda i, c: (body(i), c)[1], 0, unroll=unroll)

    copies = []
    at1 = at2 = at3 = 0
    for c in range(chunks):
        end = (c + 1) * width
        end1, end2 = min(nb, end + 4), min(nb, end + 2)
        loop(at1, end1, first, 4)
        loop(at2 // 2, end2 // 2, second, 1)
        loop(at3, end, third, 2)
        at1, at2, at3 = end1, end2, end
        cols = pl.ds(c * width * 128, width * 128)
        for n, (src, dst) in enumerate(((fbuf, fine), (cbuf, corr))):
            copies.append(
                pltpu.make_async_copy(src.at[:, :, cols], dst.at[:, :, cols], sems.at[n, c])
            )
            copies[-1].start()
    for copy in copies:
        copy.wait()


def in_vmem(x):
    return pltpu.with_memory_space_constraint(x, pltpu.VMEM)


def spec(space=pltpu.VMEM):
    return pl.BlockSpec(memory_space=space)


def params(mib):
    return pltpu.CompilerParams(vmem_limit_bytes=mib * MIB)


def shards(count, fine_state, noise):
    f32, bf16 = jnp.float32, jnp.bfloat16
    wide = fine_state.shape[2]
    nb = wide // 128
    groups = nb // 4
    vmem = pltpu.VMEM

    pairs = [(i, i + 1) for i in range(1, count - 1, 2)]
    odd = pairs + [(b, a) for a, b in pairs]
    pairs = [(i, i + 1) for i in range(0, count - 1, 2)]
    even = pairs + [(b, a) for a, b in pairs]

    m_odd, m_even, x0, f1, own, own_q = pl.pallas_call(
        functools.partial(pre_kernel, "row"),
        out_shape=(
            vmem((nb + nb // 2, 8, 128), f32),
            vmem((nb + nb // 2, 8, 128), f32),
            vmem((2, nb + 2, 24, 128), f32),
            vmem((2, nb + 2, 8, 128), f32),
            vmem((2, nb, 8, 128), f32),
            vmem((2, nb, 8, 128), f32),
        ),
        in_specs=[spec(pl.ANY), spec(pl.ANY)],
        out_specs=[spec()] * 6,
        scratch_shapes=[
            vmem((2, 16, wide), f32),
            vmem((2, 2, 16, wide), bf16),
            pltpu.SemaphoreType.DMA((2, 4)),
        ],
        compiler_params=params(20),
        name="pre",
    )(fine_state, noise)
    m_odd = lax.ppermute(m_odd, "row", odd)
    m_even = lax.ppermute(m_even, "row", even)

    start, c_odd, c_even = pl.pallas_call(
        functools.partial(coarse_start_kernel, "row"),
        out_shape=(
            vmem((groups + 2, 8, 128), f32),
            vmem((groups // 2, 8, 128), f32),
            vmem((groups // 2, 8, 128), f32),
        ),
        in_specs=[spec()],
        out_specs=[spec()] * 3,
        scratch_shapes=[vmem((4, groups, 8, 128), f32)],
        compiler_params=params(20),
        name="coarse_start",
    )(in_vmem(x0))
    c_odd = lax.ppermute(c_odd, "row", odd)
    c_even = lax.ppermute(c_even, "row", even)

    p2, p3, n2 = pl.pallas_call(
        inner_kernel,
        out_shape=(
            vmem((2, nb, 8, 128), f32),
            vmem((2, nb, 8, 128), f32),
            vmem((2, nb, 8, 128), f32),
        ),
        in_specs=[spec()] * 3,
        out_specs=[spec()] * 3,
        scratch_shapes=[vmem((2, nb + 2, 8, 128), f32)] * 2,
        compiler_params=params(20),
        name="inner",
    )(in_vmem(x0), in_vmem(f1), noise)

    coarse, spread = pl.pallas_call(
        functools.partial(coarse_kernel, "row"),
        out_shape=(
            jax.ShapeDtypeStruct((2, 4, groups * 128), f32),
            vmem((nb, 4, 8, 128), f32),
        ),
        in_specs=[spec()] * 4,
        out_specs=[spec()] * 2,
        scratch_shapes=[vmem((4, groups, 8, 128), f32), vmem((groups, 8, 128), f32)],
        compiler_params=params(20),
        name="coarse",
    )(in_vmem(start), noise, in_vmem(c_odd), in_vmem(c_even))

    fine, corr = pl.pallas_call(
        functools.partial(post_kernel, "row"),
        out_shape=(
            jax.ShapeDtypeStruct((2, 16, wide), f32),
            jax.ShapeDtypeStruct((2, 16, wide), f32),
        ),
        in_specs=[spec()] * 8,
        out_specs=[spec(pl.ANY)] * 2,
        scratch_shapes=[
            vmem((2, nb + 2, 24, 128), f32),
            vmem((2, nb + 2, 16, 128), f32),
            vmem((2, 16, wide), f32),
            vmem((2, 16, wide), f32),
            pltpu.SemaphoreType.DMA((2, 4)),
        ],
        compiler_params=params(24),
        name="post",
    )(*(in_vmem(x) for x in (m_odd, m_even, own, own_q, p2, p3, n2, spread)))
    return fine, coarse, corr


def solution(mesh):
    rows = P("sample", "row", None)
    return jax.shard_map(
        functools.partial(shards, mesh.shape["row"]),
        mesh=mesh,
        in_specs=(rows, P("sample", None, "row", None)),
        out_specs=(rows, rows, rows),
        check_vma=False,
    )
```

```python
import functools

import jax
import jax.numpy as jnp
from jax import lax
from jax.experimental import pallas as pl
from jax.experimental.pallas import tpu as pltpu
from jax.sharding import PartitionSpec as P

NEAR, FAR = 4.0 / 3.0, -1.0 / 12.0
DIFFUSE = (0.15, 0.05)
MIB = 1 << 20
CHUNKS = 4


def iota(dim):
    return lax.broadcasted_iota(jnp.int32, (8, 128), dim)


def pick(x, index):
    return jnp.take_along_axis(x, index, axis=0, mode="promise_in_bounds")


def turn(x, steps):
    return pltpu.roll(x, steps, 0)


def sideways(mid, left, right, lane):
    near = pltpu.roll(jnp.where(lane == 127, left, mid), 1, 1) + pltpu.roll(
        jnp.where(lane == 0, right, mid), 127, 1
    )
    far = pltpu.roll(jnp.where(lane >= 126, left, mid), 2, 1) + pltpu.roll(
        jnp.where(lane < 2, right, mid), 126, 1
    )
    return near, far


def stepped(a, b, near, far, force, scale, react):
    da, db = DIFFUSE[0] * scale, DIFFUSE[1] * scale
    new_a = a * ((1.0 + react - 5.0 * da) - (react / 3.0) * (a * a)) - react * b
    new_a = new_a + (da * NEAR) * near[0] + (da * FAR) * far[0] + force[0]
    low = 0.08 * react
    new_b = b * (1.0 - 5.0 * db - 0.8 * low) + low * a + 0.7 * low
    new_b = new_b + (db * NEAR) * near[1] + (db * FAR) * far[1] + force[1]
    return new_a, new_b


def both_ends(block, first, sub):
    block = block.astype(jnp.float32)
    half = sub >> 1
    top = pick(block[0:8], half + first)
    low = pick(block[8:16], 7 - first - half)
    return jnp.where((sub & 1) == 0, top, low)


def loop(lo, hi, body, unroll):
    if hi > lo:
        lax.fori_loop(lo, hi, lambda i, c: (body(i), c)[1], 0, unroll=unroll)


def whole_part(length, most):
    return max((d for d in range(1, most + 1) if length % d == 0), default=1)


def block_columns(j):
    return pl.ds(pl.multiple_of(j * 128, 128), 128)


def selection(k, value, transpose):
    shape = (256, 128)
    row = lax.broadcasted_iota(jnp.int32, shape, 0) & 127
    col = lax.broadcasted_iota(jnp.int32, shape, 1)
    fine, coarse = (col, row) if transpose else (row, col)
    return jnp.where(coarse == 32 * k + (fine >> 2), value, 0.0).astype(jnp.bfloat16)


def in_two(x):
    high = x.astype(jnp.bfloat16)
    low = (x - high.astype(jnp.float32)).astype(jnp.bfloat16)
    return jnp.concatenate([high, low], axis=1)


def lanes_averaged(held):
    groups = held.shape[1]
    total = jnp.zeros((groups * 8, 128), jnp.float32)
    for k in range(4):
        total = total + jnp.dot(
            in_two(held[k].reshape(groups * 8, 128)),
            selection(k, 1.0 / 16.0, False),
            preferred_element_type=jnp.float32,
        )
    return total.reshape(groups, 8, 128)


def edge_rows(parity, split, x0, noise, m_odd, m_even, f1, own, own_q):
    sub, lane = iota(0), iota(1)
    strong = [jnp.where((sub & 6) == 2, DIFFUSE[f] * NEAR, 0.0) for f in range(2)]
    wins_at = [6 - 2 * (sub & 3) + side for side in (parity, 1 - parity)]
    qs_at = [2 - 2 * (sub & 1) + side for side in (parity, 1 - parity)]

    def step(j):
        cols = block_columns(j)
        jj = j + 1
        mids, nears, fars, forces, rims = [], [], [], [], []
        for f in range(2):
            mid, up1 = x0[f, jj, 8:16], x0[f, jj, 6:14]
            near, far = sideways(mid, x0[f, jj - 1, 8:16], x0[f, jj + 1, 8:16], lane)
            nears.append(near + (up1 + x0[f, jj, 10:18]))
            fars.append(far + (x0[f, jj, 4:12] + x0[f, jj, 12:20]))
            forces.append(0.25 * both_ends(noise[0, f, :, cols], 0, sub))
            mids.append(mid)
            rims.append((DIFFUSE[f] * NEAR) * up1 + (DIFFUSE[f] * FAR) * mid)
        new = stepped(mids[0], mids[1], nears, fars, forces, 1.0, 0.05)
        wins, qs = [], []
        for f in range(2):
            half = turn(new[f], 4)
            f1[f, jj] = new[f]
            win = jnp.where(sub < 4, rims[f], half)
            own[f, j] = win
            q = 0.25 * both_ends(noise[1, f, :, cols], 0, sub)
            q = q + (DIFFUSE[f] * FAR) * half + strong[f] * turn(new[f], 6)
            own_q[f, j] = turn(q, 4)
            wins.append(win)
            qs.append(q)
        return wins, qs

    def pair(i):
        wins0, qs0 = step(2 * i)
        wins1, qs1 = step(2 * i + 1)
        base = split[0]
        blocks = split[1] - split[0]
        for n, out in enumerate((m_odd, m_even)):
            at = wins_at[n]
            k = 2 * i - base
            out[k] = jnp.where(sub < 4, pick(wins0[0], at), pick(wins0[1], at))
            out[k + 1] = jnp.where(sub < 4, pick(wins1[0], at), pick(wins1[1], at))
            at = qs_at[n]
            first = jnp.where((sub & 2) == 0, pick(qs0[0], at), pick(qs0[1], at))
            second = jnp.where((sub & 2) == 0, pick(qs1[0], at), pick(qs1[1], at))
            out[blocks + i - base // 2] = jnp.where(sub < 4, first, second)

    loop(split[0] // 2, split[1] // 2, pair, 8)


def start_kernel(
    row_axis, split, f_hbm, n_hbm, m_odd, m_even, x0, f1, own, own_q, start, noise, fbuf, held, sems
):
    nb = x0.shape[1] - 2
    groups = nb // 4
    width = nb // CHUNKS
    first, rest = [], []
    for c in range(CHUNKS):
        cols = pl.ds(c * width * 128, width * 128)
        first.append(pltpu.make_async_copy(f_hbm.at[:, :, cols], fbuf.at[:, :, cols], sems.at[c]))
    sooner, later = pl.ds(0, split * 128), pl.ds(split * 128, (nb - split) * 128)
    early = pltpu.make_async_copy(
        n_hbm.at[0:2, :, :, sooner], noise.at[0:2, :, :, sooner], sems.at[CHUNKS]
    )
    rest.append(
        pltpu.make_async_copy(
            n_hbm.at[0:2, :, :, later], noise.at[0:2, :, :, later], sems.at[CHUNKS + 1]
        )
    )
    rest.append(pltpu.make_async_copy(n_hbm.at[2:3], noise.at[2:3], sems.at[CHUNKS + 2]))
    for copy in first + [early] + rest:
        copy.start()
    sub = iota(0)
    half = sub >> 1
    parity = lax.rem(lax.axis_index(row_axis), 2)
    zero = jnp.zeros((8, 128), jnp.float32)
    for f in range(2):
        for edge in (0, nb + 1):
            for r in range(3):
                x0[f, edge, 8 * r : 8 * r + 8] = zero
            f1[f, edge] = zero
    start[0] = zero
    start[groups + 1] = zero

    def block(j):
        cols = block_columns(j)
        sums = []
        for f in range(2):
            top, low = fbuf[f, 0:8, cols], fbuf[f, 8:16, cols]
            outer = jnp.where((sub & 1) == 0, pick(top, half), pick(low, 7 - half))
            inner = jnp.where((sub & 1) == 0, pick(top, half + 4), pick(low, 3 - half))
            x0[f, j + 1, 0:8] = zero
            x0[f, j + 1, 8:16] = outer
            x0[f, j + 1, 16:24] = inner
            parts = []
            for x in (outer, inner):
                x = x + turn(x, 4)
                parts.append(x + turn(x, 2))
            sums.append(jnp.where((sub & 3) < 2, parts[0], parts[1]))
        return jnp.where(sub < 4, sums[0], sums[1])

    def group(g):
        for k in range(4):
            held[k, g] = block(4 * g + k)

    for c in range(CHUNKS):
        first[c].wait()
        loop(c * width // 4, (c + 1) * width // 4, group, 4)
    start[1 : groups + 1] = lanes_averaged(held)
    offset = m_odd.shape[0] - groups // 2

    def message(i):
        rims = []
        for h in range(2):
            c = start[2 * i + h + 1]
            rims.append(jnp.where((sub & 2) == 0, NEAR * c, 0.0) + FAR * pick(c, sub ^ 2))
        for out, side in ((m_odd, parity), (m_even, 1 - parity)):
            at = (2 * sub + side) & 7
            out[offset + i] = jnp.where(sub < 4, pick(rims[0], at), pick(rims[1], at))

    loop(0, groups // 2, message, 8)
    early.wait()
    edge_rows(parity, (0, split), x0, noise, m_odd, m_even, f1, own, own_q)
    for copy in rest:
        copy.wait()


def edge_kernel(row_axis, split, x0, noise, f1_in, own_in, q_in, m_odd, m_even, f1, own, own_q):
    del f1_in, own_in, q_in
    parity = lax.rem(lax.axis_index(row_axis), 2)
    edge_rows(parity, (split, own.shape[1]), x0, noise, m_odd, m_even, f1, own, own_q)


def inner_kernel(x0, f1, noise, p2, p3, n2, g1, g2):
    nb = x0.shape[1] - 2
    sub, lane = iota(0), iota(1)
    zero = jnp.zeros((8, 128), jnp.float32)
    for f in range(2):
        for edge in (0, nb + 1):
            g1[f, edge] = zero
            g2[f, edge] = zero
    down1 = jnp.where(sub < 6, sub + 2, 13 - sub)
    down2 = jnp.where(sub < 4, sub + 4, 11 - sub)

    def first(j):
        cols = block_columns(j)
        jj = j + 1
        mids, nears, fars, forces = [], [], [], []
        for f in range(2):
            mid = x0[f, jj, 16:24]
            near, far = sideways(mid, x0[f, jj - 1, 16:24], x0[f, jj + 1, 16:24], lane)
            nears.append(near + (x0[f, jj, 14:22] + pick(mid, down1)))
            fars.append(far + (x0[f, jj, 12:20] + pick(mid, down2)))
            forces.append(0.25 * both_ends(noise[0, f, :, cols], 4, sub))
            mids.append(mid)
        new = stepped(mids[0], mids[1], nears, fars, forces, 1.0, 0.05)
        for f in range(2):
            g1[f, jj] = new[f]

    def second(j):
        cols = block_columns(j)
        jj = j + 1
        mids, nears, fars, forces = [], [], [], []
        tops, top_nears, top_fars, top_forces = [], [], [], []
        for f in range(2):
            mid, top = g1[f, jj], f1[f, jj]
            top2, mid2, top4, mid4 = turn(top, 2), turn(mid, 2), turn(top, 4), turn(mid, 4)
            low2 = jnp.where(sub < 4, top4, mid4)
            near, far = sideways(mid, g1[f, jj - 1], g1[f, jj + 1], lane)
            nears.append(near + (jnp.where(sub < 2, top2, mid2) + pick(mid, down1)))
            fars.append(far + (low2 + pick(mid, down2)))
            noises = noise[1, f, :, cols]
            forces.append(0.25 * both_ends(noises, 4, sub))
            mids.append(mid)
            near, far = sideways(top, f1[f, jj - 1], f1[f, jj + 1], lane)
            up1 = jnp.where(sub < 6, 0.0, top2)
            low1 = jnp.where(sub < 6, turn(top, 6), turn(mid, 6))
            top_nears.append(near + (up1 + low1))
            top_fars.append(far + low2)
            top_forces.append(0.25 * both_ends(noises, 0, sub))
            tops.append(top)
        new = stepped(mids[0], mids[1], nears, fars, forces, 1.0, 0.05)
        part = stepped(tops[0], tops[1], top_nears, top_fars, top_forces, 1.0, 0.05)
        for f in range(2):
            g2[f, jj] = new[f]
            p2[f, j] = jnp.where(sub < 4, turn(part[f], 4), turn(new[f], 4))

    def third(j):
        cols = block_columns(j)
        jj = j + 1
        mids, nears, fars, forces = [], [], [], []
        for f in range(2):
            mid = g2[f, jj]
            near, far = sideways(mid, g2[f, jj - 1], g2[f, jj + 1], lane)
            up1 = jnp.where(sub < 2, 0.0, turn(mid, 2))
            up2 = jnp.where(sub < 4, 0.0, turn(mid, 4))
            nears.append(near + (up1 + pick(mid, down1)))
            fars.append(far + (up2 + pick(mid, down2)))
            noises = noise[2, f, :, cols]
            forces.append(0.25 * both_ends(noises, 4, sub))
            n2[f, j] = 0.25 * both_ends(noises, 0, sub)
            mids.append(mid)
        new = stepped(mids[0], mids[1], nears, fars, forces, 1.0, 0.05)
        for f in range(2):
            p3[f, j] = new[f]

    loop(0, nb, first, 16)
    loop(0, nb, second, 8)
    loop(0, nb, third, 16)


def coarse_kernel(row_axis, start, noise, a_odd, a_even, coarse, spread, held, push):
    groups = start.shape[0] - 2
    offset = a_odd.shape[0] - groups // 2
    sub, lane = iota(0), iota(1)
    parity = lax.rem(lax.axis_index(row_axis), 2)
    mine = (sub & 1) == parity

    def gather_noise(g):
        for k in range(4):
            cols = block_columns(4 * g + k)
            sums = []
            for f in range(2):
                total = noise[0, f, :, cols].astype(jnp.float32)
                total = total + noise[1, f, :, cols].astype(jnp.float32)
                total = total + noise[2, f, :, cols].astype(jnp.float32)
                parts = []
                for r in (0, 8):
                    x = total[r : r + 8]
                    x = x + turn(x, 7)
                    parts.append(x + turn(x, 6))
                sums.append(
                    jnp.where(
                        (sub & 1) == 0,
                        pick(parts[0], (sub & 2) * 2),
                        pick(parts[1], 4 - (sub & 2) * 2),
                    )
                )
            held[k, g] = jnp.where(sub < 4, sums[0], sums[1])

    loop(0, groups, gather_noise, 2)
    push[...] = lanes_averaged(held)

    is_a = sub < 4
    scale, react = 3.0 / 16.0, 0.15
    diffuse = jnp.where(is_a, DIFFUSE[0] * scale, DIFFUSE[1] * scale)
    order = jnp.where(sub < 1, 0, jnp.where(sub < 2, 2, jnp.where(sub < 3, 3, 1)))
    inward = jnp.where((sub & 2) == 0, sub + 2, sub ^ 1)

    def update(i):
        odd, even = a_odd[offset + i], a_even[offset + i]
        for h in range(2):
            g = 2 * i + h
            c = start[g + 1]
            near, far = sideways(c, start[g], start[g + 2], lane)
            near = near + pick(c, inward) + jnp.where((sub & 2) == 0, 0.0, turn(c, 2))
            far = far + pick(c, (sub & 4) + 3 - (sub & 3))
            at = 4 * h + (sub >> 1)
            rim = jnp.where(mine, pick(odd, at), pick(even, at))
            lap = NEAR * near + FAR * far + rim - 5.0 * c
            other = turn(c, 4)
            change = jnp.where(
                is_a,
                react * (c - c * c * c / 3.0 - other),
                (react * 0.08) * (other + 0.7 - 0.8 * c),
            )
            new = c + diffuse * lap + change + push[g]
            push[g] = new
            cols = block_columns(g)
            for f in range(2):
                coarse[f, :, cols] = pick(new, order + 4 * f)[0:4]

    loop(0, groups // 2, update, 4)
    whole = in_two(push[...].reshape(groups * 8, 128))
    for k in range(4):
        held[k] = jnp.dot(
            whole, selection(k, 1.0, True), preferred_element_type=jnp.float32
        ).reshape(groups, 8, 128)

    def spread_rows(g):
        for k in range(4):
            x = held[k, g]
            for f in range(2):
                spread[4 * g + k, 2 * f] = pick(x, 4 * f + jnp.where(sub < 4, 0, 2))
                spread[4 * g + k, 2 * f + 1] = pick(x, 4 * f + jnp.where(sub < 4, 3, 1))

    loop(0, groups, spread_rows, 4)


def finish(
    row_axis, spans, base, m_odd, m_even, own, own_q, p2, p3, n2, spread, fine, corr, g1, g2, fbuf, cbuf, sems
):
    nb = own.shape[1]
    blocks = base[1] - base[0]
    sub, lane = iota(0), iota(1)
    place = lax.axis_index(row_axis)
    parity = lax.rem(place, 2)
    last = lax.axis_size(row_axis) - 1
    mine = (sub & 1) == parity
    outside = ((place == 0) & ((sub & 1) == 0)) | ((place == last) & ((sub & 1) == 1))
    keep = jnp.where(outside & (sub < 4), jnp.float32(0.0), jnp.float32(1.0))
    half = sub >> 1
    zero = jnp.zeros((8, 128), jnp.float32)
    close = [jnp.where(sub < 2, DIFFUSE[f] * NEAR, 0.0) for f in range(2)]
    wide = [jnp.where(sub < 4, DIFFUSE[f] * FAR, 0.0) for f in range(2)]
    even_rows = (2 * sub) & 7

    def first(i):
        qs_odd = m_odd[blocks + i - base[0] // 2]
        qs_even = m_even[blocks + i - base[0] // 2]
        for h in range(2):
            j = 2 * i + h
            odd, even = m_odd[j - base[0]], m_even[j - base[0]]
            for f in range(2):
                came = jnp.where(mine, pick(odd, half + 4 * f), pick(even, half + 4 * f))
                at = (half & 1) + (2 * f + 4 * h)
                force = jnp.where(mine, pick(qs_odd, at), pick(qs_even, at))
                g1[f, j + 1, 0:8] = zero
                g1[f, j + 1, 8:16] = (came + own[f, j]) * keep
                g1[f, j + 1, 16:24] = jnp.where(sub < 4, force, own_q[f, j])

    def second(j):
        jj = j + 1
        mids, nears, fars, forces = [], [], [], []
        for f in range(2):
            mid = g1[f, jj, 8:16]
            near, far = sideways(mid, g1[f, jj - 1, 8:16], g1[f, jj + 1, 8:16], lane)
            turned = turn(mid, 4)
            up = turn(mid, 2)
            nears.append(near + (g1[f, jj, 6:14] + jnp.where(sub < 6, turn(mid, 6), 0.0)))
            fars.append(far + turned)
            forces.append(g1[f, jj, 16:24])
            mids.append(mid)
            g2[f, jj, 8:16] = p2[f, j] + (close[f] * up + wide[f] * turned)
        new = stepped(mids[0], mids[1], nears, fars, forces, 1.0, 0.05)
        for f in range(2):
            g2[f, jj, 0:8] = new[f] * keep

    def third(j):
        cols = block_columns(j)
        jj = j + 1
        mids, nears, fars, forces, deep = [], [], [], [], []
        for f in range(2):
            mid = g2[f, jj, 4:12]
            low2 = g2[f, jj, 8:16]
            near, far = sideways(mid, g2[f, jj - 1, 4:12], g2[f, jj + 1, 4:12], lane)
            nears.append(near + (g2[f, jj, 2:10] + g2[f, jj, 6:14]))
            fars.append(far + (g2[f, jj, 0:8] + low2))
            forces.append(n2[f, j])
            mids.append(mid)
            deep.append(p3[f, j] + (close[f] * turn(low2, 6) + wide[f] * low2))
        new = stepped(mids[0], mids[1], nears, fars, forces, 1.0, 0.05)
        for f in range(2):
            top = jnp.where(sub < 4, pick(new[f], even_rows), pick(deep[f], even_rows))
            low = jnp.where(sub < 4, pick(deep[f], 7 - even_rows), pick(new[f], 7 - even_rows))
            fbuf[f, 0:8, cols] = top
            fbuf[f, 8:16, cols] = low
            cbuf[f, 0:8, cols] = top - spread[j, 2 * f]
            cbuf[f, 8:16, cols] = low - spread[j, 2 * f + 1]

    for f in range(2):
        for edge in (0, nb + 1):
            for r in range(3):
                g1[f, edge, 8 * r : 8 * r + 8] = zero
            for r in range(2):
                g2[f, edge, 8 * r : 8 * r + 8] = zero
    copies = []
    for c, (span1, span2, span3) in enumerate(spans):
        loop(span1[0] // 2, span1[1] // 2, first, whole_part((span1[1] - span1[0]) // 2, 8))
        loop(*span2, second, whole_part(span2[1] - span2[0], 22))
        loop(*span3, third, whole_part(span3[1] - span3[0], 22))
        cols = pl.ds(span3[0] * 128, (span3[1] - span3[0]) * 128)
        for n, (src, dst) in enumerate(((fbuf, fine), (cbuf, corr))):
            copies.append(
                pltpu.make_async_copy(src.at[:, :, cols], dst.at[:, :, cols], sems.at[n, c])
            )
            copies[-1].start()
    for copy in copies:
        copy.wait()


def early_kernel(row_axis, split, *refs):
    ins, outs, carried, scratch = refs[:8], refs[8:10], refs[10:12], refs[12:]
    g1, g2 = scratch[:2]
    mid = split // 2
    spans = [
        ((0, split), (0, split - 1), (0, mid)),
        ((split, split), (split - 1, split - 1), (mid, split - 2)),
    ]
    finish(row_axis, spans, (0, split), *ins, *outs, *scratch)
    for f in range(2):
        for k in range(2):
            for r in range(3):
                carried[0][f, k, 8 * r : 8 * r + 8] = g1[f, split - 1 + k, 8 * r : 8 * r + 8]
            for r in range(2):
                carried[1][f, k, 8 * r : 8 * r + 8] = g2[f, split - 2 + k, 8 * r : 8 * r + 8]


def late_kernel(row_axis, split, *refs):
    ins, carried, outs, scratch = refs[:8], refs[8:10], refs[12:14], refs[14:]
    g1, g2 = scratch[:2]
    nb = ins[2].shape[1]
    for f in range(2):
        for k in range(2):
            for r in range(3):
                g1[f, split - 1 + k, 8 * r : 8 * r + 8] = carried[0][f, k, 8 * r : 8 * r + 8]
            for r in range(2):
                g2[f, split - 2 + k, 8 * r : 8 * r + 8] = carried[1][f, k, 8 * r : 8 * r + 8]
    mid = split + (nb - split) // 2
    spans = [
        ((split, nb), (split - 1, nb), (split - 2, mid)),
        ((nb, nb), (nb, nb), (mid, nb)),
    ]
    finish(row_axis, spans, (split, nb), *ins, *outs, *scratch)


def in_vmem(x):
    return pltpu.with_memory_space_constraint(x, pltpu.VMEM)


def in_hbm(x):
    return pltpu.with_memory_space_constraint(x, pltpu.HBM)


def spec(space):
    return pl.BlockSpec(memory_space=space)


def call(kernel, name, mib, ins, outs, scratch, hbm_ins=(), hbm_outs=(), aliases=None):
    return pl.pallas_call(
        kernel,
        out_shape=tuple(hbm_outs) + tuple(outs),
        in_specs=[spec(pltpu.VMEM)] * len(ins) + [spec(pltpu.HBM)] * len(hbm_ins),
        out_specs=(spec(pltpu.HBM),) * len(hbm_outs) + (spec(pltpu.VMEM),) * len(outs),
        scratch_shapes=scratch,
        input_output_aliases=aliases or {},
        compiler_params=pltpu.CompilerParams(vmem_limit_bytes=mib * MIB),
        name=name,
    )(*(in_vmem(x) for x in ins), *(in_hbm(x) for x in hbm_ins))


def shards(count, fine_state, noise):
    f32 = jnp.float32
    wide = fine_state.shape[2]
    nb = wide // 128
    groups = nb // 4
    split = nb // 2

    def vmem(*shape):
        return pltpu.VMEM(shape, f32)

    pairs = [(i, i + 1) for i in range(1, count - 1, 2)]
    odd = pairs + [(b, a) for a, b in pairs]
    pairs = [(i, i + 1) for i in range(0, count - 1, 2)]
    even = pairs + [(b, a) for a, b in pairs]

    a_rows = split + split // 2 + groups // 2
    a_odd, a_even, x0, f1, own, own_q, start, held_noise = call(
        functools.partial(start_kernel, "row", split),
        "start",
        16,
        [],
        [
            vmem(a_rows, 8, 128),
            vmem(a_rows, 8, 128),
            vmem(2, nb + 2, 24, 128),
            vmem(2, nb + 2, 8, 128),
            vmem(2, nb, 8, 128),
            vmem(2, nb, 8, 128),
            vmem(groups + 2, 8, 128),
            pltpu.VMEM(noise.shape, noise.dtype),
        ],
        [vmem(2, 16, wide), vmem(4, groups, 8, 128), pltpu.SemaphoreType.DMA((CHUNKS + 3,))],
        hbm_ins=[fine_state, noise],
    )
    a_odd = lax.ppermute(a_odd, "row", odd)
    a_even = lax.ppermute(a_even, "row", even)

    b_rows = (nb - split) + (nb - split) // 2
    b_odd, b_even, f1, own, own_q = call(
        functools.partial(edge_kernel, "row", split),
        "edge",
        16,
        [x0, held_noise, f1, own, own_q],
        [
            vmem(b_rows, 8, 128),
            vmem(b_rows, 8, 128),
            vmem(2, nb + 2, 8, 128),
            vmem(2, nb, 8, 128),
            vmem(2, nb, 8, 128),
        ],
        [],
        aliases={2: 2, 3: 3, 4: 4},
    )
    b_odd = lax.ppermute(b_odd, "row", odd)
    b_even = lax.ppermute(b_even, "row", even)

    p2, p3, n2 = call(
        inner_kernel,
        "inner",
        16,
        [x0, f1, held_noise],
        [vmem(2, nb, 8, 128)] * 3,
        [vmem(2, nb + 2, 8, 128)] * 2,
    )
    coarse, spread = call(
        functools.partial(coarse_kernel, "row"),
        "coarse",
        16,
        [start, held_noise, a_odd, a_even],
        [jax.ShapeDtypeStruct((2, 4, groups * 128), f32), vmem(nb, 4, 8, 128)],
        [vmem(4, groups, 8, 128), vmem(groups, 8, 128)],
    )
    work = [
        vmem(2, nb + 2, 24, 128),
        vmem(2, nb + 2, 16, 128),
        vmem(2, 16, wide),
        vmem(2, 16, wide),
        pltpu.SemaphoreType.DMA((2, 2)),
    ]
    whole = [jax.ShapeDtypeStruct((2, 16, wide), f32)] * 2
    fine, corr, last1, last2 = call(
        functools.partial(early_kernel, "row", split),
        "early",
        16,
        [a_odd, a_even, own, own_q, p2, p3, n2, spread],
        [vmem(2, 2, 24, 128), vmem(2, 2, 16, 128)],
        work,
        hbm_outs=whole,
    )
    fine, corr = call(
        functools.partial(late_kernel, "row", split),
        "late",
        16,
        [b_odd, b_even, own, own_q, p2, p3, n2, spread, last1, last2],
        [],
        work,
        hbm_ins=[fine, corr],
        hbm_outs=whole,
        aliases={10: 0, 11: 1},
    )
    return fine, coarse, corr


def solution(mesh):
    rows = P("sample", "row", None)
    return jax.shard_map(
        functools.partial(shards, mesh.shape["row"]),
        mesh=mesh,
        in_specs=(rows, P("sample", None, "row", None)),
        out_specs=(rows, rows, rows),
        check_vma=False,
    )
```

```python
import functools

import jax
import jax.numpy as jnp
from jax import lax
from jax.experimental import pallas as pl
from jax.experimental.pallas import tpu as pltpu
from jax.sharding import PartitionSpec as P

NEAR, FAR = 4.0 / 3.0, -1.0 / 12.0
DIFFUSE = (0.15, 0.05)
MIB = 1 << 20
CHUNKS = 8
MOST = 48


def iota(dim):
    return lax.broadcasted_iota(jnp.int32, (8, 128), dim)


def pick(x, index):
    return jnp.take_along_axis(x, index, axis=0, mode="promise_in_bounds")


def turn(x, steps):
    return pltpu.roll(x, steps, 0)


def sideways(mid, left, right, lane):
    near = pltpu.roll(jnp.where(lane == 127, left, mid), 1, 1) + pltpu.roll(
        jnp.where(lane == 0, right, mid), 127, 1
    )
    far = pltpu.roll(jnp.where(lane >= 126, left, mid), 2, 1) + pltpu.roll(
        jnp.where(lane < 2, right, mid), 126, 1
    )
    return near, far


def stepped(a, b, near, far, force, scale, react):
    da, db = DIFFUSE[0] * scale, DIFFUSE[1] * scale
    new_a = a * ((1.0 + react - 5.0 * da) - (react / 3.0) * (a * a)) - react * b
    new_a = new_a + (da * NEAR) * near[0] + (da * FAR) * far[0] + force[0]
    low = 0.08 * react
    new_b = b * (1.0 - 5.0 * db - 0.8 * low) + low * a + 0.7 * low
    new_b = new_b + (db * NEAR) * near[1] + (db * FAR) * far[1] + force[1]
    return new_a, new_b


def both_ends(block, first, sub):
    block = block.astype(jnp.float32)
    half = sub >> 1
    top = pick(block[0:8], half + first)
    low = pick(block[8:16], 7 - first - half)
    return jnp.where((sub & 1) == 0, top, low)


def loop(lo, hi, body, unroll):
    if hi > lo:
        lax.fori_loop(lo, hi, lambda i, c: (body(i), c)[1], 0, unroll=unroll)


def long_loop(lo, hi, body, most):
    if hi <= lo:
        return
    steps = -(-(hi - lo) // most)
    each = (hi - lo) // steps
    last = lo + (steps - 1) * each
    loop(lo, last, body, each)
    for j in range(last, hi):
        body(j)


def block_columns(j):
    return pl.ds(pl.multiple_of(j * 128, 128), 128)


def selection(k, value, transpose):
    shape = (256, 128)
    row = lax.broadcasted_iota(jnp.int32, shape, 0) & 127
    col = lax.broadcasted_iota(jnp.int32, shape, 1)
    fine, coarse = (col, row) if transpose else (row, col)
    return jnp.where(coarse == 32 * k + (fine >> 2), value, 0.0).astype(jnp.bfloat16)


def in_two(x):
    high = x.astype(jnp.bfloat16)
    low = (x - high.astype(jnp.float32)).astype(jnp.bfloat16)
    return jnp.concatenate([high, low], axis=1)


def lanes_averaged(held):
    groups = held.shape[1]
    total = jnp.zeros((groups * 8, 128), jnp.float32)
    for k in range(4):
        total = total + jnp.dot(
            in_two(held[k].reshape(groups * 8, 128)),
            selection(k, 1.0 / 16.0, False),
            preferred_element_type=jnp.float32,
        )
    return total.reshape(groups, 8, 128)


def edge_rows(parity, split, x0, noise, m_odd, m_even, f1, own, own_q):
    sub, lane = iota(0), iota(1)
    strong = [jnp.where((sub & 6) == 2, DIFFUSE[f] * NEAR, 0.0) for f in range(2)]
    wins_at = [6 - 2 * (sub & 3) + side for side in (parity, 1 - parity)]
    qs_at = [2 - 2 * (sub & 1) + side for side in (parity, 1 - parity)]

    def step(j):
        cols = block_columns(j)
        jj = j + 1
        mids, nears, fars, forces, rims = [], [], [], [], []
        for f in range(2):
            mid, up1 = x0[f, jj, 8:16], x0[f, jj, 6:14]
            near, far = sideways(mid, x0[f, jj - 1, 8:16], x0[f, jj + 1, 8:16], lane)
            nears.append(near + (up1 + x0[f, jj, 10:18]))
            fars.append(far + (x0[f, jj, 4:12] + x0[f, jj, 12:20]))
            forces.append(0.25 * both_ends(noise[0, f, :, cols], 0, sub))
            mids.append(mid)
            rims.append((DIFFUSE[f] * NEAR) * up1 + (DIFFUSE[f] * FAR) * mid)
        new = stepped(mids[0], mids[1], nears, fars, forces, 1.0, 0.05)
        wins, qs = [], []
        for f in range(2):
            half = turn(new[f], 4)
            f1[f, jj] = new[f]
            win = jnp.where(sub < 4, rims[f], half)
            own[f, j] = win
            q = 0.25 * both_ends(noise[1, f, :, cols], 0, sub)
            q = q + (DIFFUSE[f] * FAR) * half + strong[f] * turn(new[f], 6)
            own_q[f, j] = turn(q, 4)
            wins.append(win)
            qs.append(q)
        return wins, qs

    def pair(i):
        wins0, qs0 = step(2 * i)
        wins1, qs1 = step(2 * i + 1)
        base = split[0]
        blocks = split[1] - split[0]
        for n, out in enumerate((m_odd, m_even)):
            at = wins_at[n]
            k = 2 * i - base
            out[k] = jnp.where(sub < 4, pick(wins0[0], at), pick(wins0[1], at))
            out[k + 1] = jnp.where(sub < 4, pick(wins1[0], at), pick(wins1[1], at))
            at = qs_at[n]
            first = jnp.where((sub & 2) == 0, pick(qs0[0], at), pick(qs0[1], at))
            second = jnp.where((sub & 2) == 0, pick(qs1[0], at), pick(qs1[1], at))
            out[blocks + i - base // 2] = jnp.where(sub < 4, first, second)

    long_loop(split[0] // 2, split[1] // 2, pair, 18)


def start_kernel(
    row_axis, split, f_hbm, n_hbm, m_odd, m_even, x0, f1, own, own_q, start, noise, fbuf, held, sems
):
    nb = x0.shape[1] - 2
    groups = nb // 4
    width = nb // CHUNKS
    first, rest = [], []
    for c in range(CHUNKS):
        cols = pl.ds(c * width * 128, width * 128)
        first.append(pltpu.make_async_copy(f_hbm.at[:, :, cols], fbuf.at[:, :, cols], sems.at[c]))
    sooner, later = pl.ds(0, split * 128), pl.ds(split * 128, (nb - split) * 128)
    early = pltpu.make_async_copy(
        n_hbm.at[0:2, :, :, sooner], noise.at[0:2, :, :, sooner], sems.at[CHUNKS]
    )
    rest.append(
        pltpu.make_async_copy(
            n_hbm.at[0:2, :, :, later], noise.at[0:2, :, :, later], sems.at[CHUNKS + 1]
        )
    )
    rest.append(pltpu.make_async_copy(n_hbm.at[2:3], noise.at[2:3], sems.at[CHUNKS + 2]))
    for copy in first + [early] + rest:
        copy.start()
    sub = iota(0)
    half = sub >> 1
    parity = lax.rem(lax.axis_index(row_axis), 2)
    zero = jnp.zeros((8, 128), jnp.float32)
    for f in range(2):
        for edge in (0, nb + 1):
            for r in range(3):
                x0[f, edge, 8 * r : 8 * r + 8] = zero
            f1[f, edge] = zero
    start[0] = zero
    start[groups + 1] = zero

    def block(j):
        cols = block_columns(j)
        sums = []
        for f in range(2):
            top, low = fbuf[f, 0:8, cols], fbuf[f, 8:16, cols]
            outer = jnp.where((sub & 1) == 0, pick(top, half), pick(low, 7 - half))
            inner = jnp.where((sub & 1) == 0, pick(top, half + 4), pick(low, 3 - half))
            x0[f, j + 1, 0:8] = zero
            x0[f, j + 1, 8:16] = outer
            x0[f, j + 1, 16:24] = inner
            parts = []
            for x in (outer, inner):
                x = x + turn(x, 4)
                parts.append(x + turn(x, 2))
            sums.append(jnp.where((sub & 3) < 2, parts[0], parts[1]))
        return jnp.where(sub < 4, sums[0], sums[1])

    def group(g):
        for k in range(4):
            held[k, g] = block(4 * g + k)

    for c in range(CHUNKS):
        first[c].wait()
        loop(c * width // 4, (c + 1) * width // 4, group, 4)
    start[1 : groups + 1] = lanes_averaged(held)
    offset = m_odd.shape[0] - groups // 2

    def message(i):
        rims = []
        for h in range(2):
            c = start[2 * i + h + 1]
            rims.append(jnp.where((sub & 2) == 0, NEAR * c, 0.0) + FAR * pick(c, sub ^ 2))
        for out, side in ((m_odd, parity), (m_even, 1 - parity)):
            at = (2 * sub + side) & 7
            out[offset + i] = jnp.where(sub < 4, pick(rims[0], at), pick(rims[1], at))

    loop(0, groups // 2, message, 8)
    early.wait()
    edge_rows(parity, (0, split), x0, noise, m_odd, m_even, f1, own, own_q)
    for copy in rest:
        copy.wait()


def edge_kernel(row_axis, split, x0, noise, f1_in, own_in, q_in, m_odd, m_even, f1, own, own_q):
    del f1_in, own_in, q_in
    parity = lax.rem(lax.axis_index(row_axis), 2)
    edge_rows(parity, (split, own.shape[1]), x0, noise, m_odd, m_even, f1, own, own_q)


def inner_kernel(x0, f1, noise, start, p2, p3, n2, part, g1, g2, held):
    nb = x0.shape[1] - 2
    sub, lane = iota(0), iota(1)
    zero = jnp.zeros((8, 128), jnp.float32)
    for f in range(2):
        for edge in (0, nb + 1):
            g1[f, edge] = zero
            g2[f, edge] = zero
    down1 = jnp.where(sub < 6, sub + 2, 13 - sub)
    down2 = jnp.where(sub < 4, sub + 4, 11 - sub)

    def first(j):
        cols = block_columns(j)
        jj = j + 1
        mids, nears, fars, forces = [], [], [], []
        for f in range(2):
            mid = x0[f, jj, 16:24]
            near, far = sideways(mid, x0[f, jj - 1, 16:24], x0[f, jj + 1, 16:24], lane)
            nears.append(near + (x0[f, jj, 14:22] + pick(mid, down1)))
            fars.append(far + (x0[f, jj, 12:20] + pick(mid, down2)))
            forces.append(0.25 * both_ends(noise[0, f, :, cols], 4, sub))
            mids.append(mid)
        new = stepped(mids[0], mids[1], nears, fars, forces, 1.0, 0.05)
        for f in range(2):
            g1[f, jj] = new[f]

    def second(j):
        cols = block_columns(j)
        jj = j + 1
        mids, nears, fars, forces = [], [], [], []
        tops, top_nears, top_fars, top_forces = [], [], [], []
        for f in range(2):
            mid, top = g1[f, jj], f1[f, jj]
            top2, mid2, top4, mid4 = turn(top, 2), turn(mid, 2), turn(top, 4), turn(mid, 4)
            low2 = jnp.where(sub < 4, top4, mid4)
            near, far = sideways(mid, g1[f, jj - 1], g1[f, jj + 1], lane)
            nears.append(near + (jnp.where(sub < 2, top2, mid2) + pick(mid, down1)))
            fars.append(far + (low2 + pick(mid, down2)))
            noises = noise[1, f, :, cols]
            forces.append(0.25 * both_ends(noises, 4, sub))
            mids.append(mid)
            near, far = sideways(top, f1[f, jj - 1], f1[f, jj + 1], lane)
            up1 = jnp.where(sub < 6, 0.0, top2)
            low1 = jnp.where(sub < 6, turn(top, 6), turn(mid, 6))
            top_nears.append(near + (up1 + low1))
            top_fars.append(far + low2)
            top_forces.append(0.25 * both_ends(noises, 0, sub))
            tops.append(top)
        new = stepped(mids[0], mids[1], nears, fars, forces, 1.0, 0.05)
        part = stepped(tops[0], tops[1], top_nears, top_fars, top_forces, 1.0, 0.05)
        for f in range(2):
            g2[f, jj] = new[f]
            p2[f, j] = jnp.where(sub < 4, turn(part[f], 4), turn(new[f], 4))

    def third(j):
        cols = block_columns(j)
        jj = j + 1
        mids, nears, fars, forces = [], [], [], []
        for f in range(2):
            mid = g2[f, jj]
            near, far = sideways(mid, g2[f, jj - 1], g2[f, jj + 1], lane)
            up1 = jnp.where(sub < 2, 0.0, turn(mid, 2))
            up2 = jnp.where(sub < 4, 0.0, turn(mid, 4))
            nears.append(near + (up1 + pick(mid, down1)))
            fars.append(far + (up2 + pick(mid, down2)))
            noises = noise[2, f, :, cols]
            forces.append(0.25 * both_ends(noises, 4, sub))
            n2[f, j] = 0.25 * both_ends(noises, 0, sub)
            mids.append(mid)
        new = stepped(mids[0], mids[1], nears, fars, forces, 1.0, 0.05)
        for f in range(2):
            p3[f, j] = new[f]

    loop(0, nb, first, 32)
    loop(0, nb, second, 32)
    loop(0, nb, third, 32)
    coarse_alone(start, noise, part, held)


def coarse_alone(start, noise, part, held):
    groups = part.shape[0]
    sub, lane = iota(0), iota(1)

    def gather_noise(g):
        for k in range(4):
            cols = block_columns(4 * g + k)
            sums = []
            for f in range(2):
                total = noise[0, f, :, cols].astype(jnp.float32)
                total = total + noise[1, f, :, cols].astype(jnp.float32)
                total = total + noise[2, f, :, cols].astype(jnp.float32)
                parts = []
                for r in (0, 8):
                    x = total[r : r + 8]
                    x = x + turn(x, 7)
                    parts.append(x + turn(x, 6))
                sums.append(
                    jnp.where(
                        (sub & 1) == 0,
                        pick(parts[0], (sub & 2) * 2),
                        pick(parts[1], 4 - (sub & 2) * 2),
                    )
                )
            held[k, g] = jnp.where(sub < 4, sums[0], sums[1])

    loop(0, groups, gather_noise, 4)
    part[...] = lanes_averaged(held)

    is_a = sub < 4
    scale, react = 3.0 / 16.0, 0.15
    diffuse = jnp.where(is_a, DIFFUSE[0] * scale, DIFFUSE[1] * scale)
    inward = jnp.where((sub & 2) == 0, sub + 2, sub ^ 1)

    def update(g):
        c = start[g + 1]
        near, far = sideways(c, start[g], start[g + 2], lane)
        near = near + pick(c, inward) + jnp.where((sub & 2) == 0, 0.0, turn(c, 2))
        far = far + pick(c, (sub & 4) + 3 - (sub & 3))
        lap = NEAR * near + FAR * far - 5.0 * c
        other = turn(c, 4)
        change = jnp.where(
            is_a,
            react * (c - c * c * c / 3.0 - other),
            (react * 0.08) * (other + 0.7 - 0.8 * c),
        )
        part[g] = c + diffuse * lap + change + part[g]

    loop(0, groups, update, 16)


def coarse_kernel(row_axis, part, a_odd, a_even, coarse, spread, held, new):
    groups = part.shape[0]
    offset = a_odd.shape[0] - groups // 2
    sub = iota(0)
    parity = lax.rem(lax.axis_index(row_axis), 2)
    mine = (sub & 1) == parity
    scale = 3.0 / 16.0
    diffuse = jnp.where(sub < 4, DIFFUSE[0] * scale, DIFFUSE[1] * scale)
    order = jnp.where(sub < 1, 0, jnp.where(sub < 2, 2, jnp.where(sub < 3, 3, 1)))

    def add_rim(i):
        odd, even = a_odd[offset + i], a_even[offset + i]
        for h in range(2):
            g = 2 * i + h
            at = 4 * h + (sub >> 1)
            rim = jnp.where(mine, pick(odd, at), pick(even, at))
            whole = part[g] + diffuse * rim
            new[g] = whole
            cols = block_columns(g)
            for f in range(2):
                coarse[f, :, cols] = pick(whole, order + 4 * f)[0:4]

    loop(0, groups // 2, add_rim, 8)
    whole = in_two(new[...].reshape(groups * 8, 128))
    for k in range(4):
        held[k] = jnp.dot(
            whole, selection(k, 1.0, True), preferred_element_type=jnp.float32
        ).reshape(groups, 8, 128)

    def spread_rows(g):
        for k in range(4):
            x = held[k, g]
            for f in range(2):
                spread[4 * g + k, 2 * f] = pick(x, 4 * f + jnp.where(sub < 4, 0, 2))
                spread[4 * g + k, 2 * f + 1] = pick(x, 4 * f + jnp.where(sub < 4, 3, 1))

    loop(0, groups, spread_rows, 8)


def finish(
    row_axis, spans, base, m_odd, m_even, own, own_q, p2, p3, n2, spread, fine, corr, g1, g2, fbuf, cbuf, sems
):
    nb = own.shape[1]
    blocks = base[1] - base[0]
    sub, lane = iota(0), iota(1)
    place = lax.axis_index(row_axis)
    parity = lax.rem(place, 2)
    last = lax.axis_size(row_axis) - 1
    mine = (sub & 1) == parity
    outside = ((place == 0) & ((sub & 1) == 0)) | ((place == last) & ((sub & 1) == 1))
    keep = jnp.where(outside & (sub < 4), jnp.float32(0.0), jnp.float32(1.0))
    half = sub >> 1
    zero = jnp.zeros((8, 128), jnp.float32)
    close = [jnp.where(sub < 2, DIFFUSE[f] * NEAR, 0.0) for f in range(2)]
    wide = [jnp.where(sub < 4, DIFFUSE[f] * FAR, 0.0) for f in range(2)]
    even_rows = (2 * sub) & 7

    def first(i):
        qs_odd = m_odd[blocks + i - base[0] // 2]
        qs_even = m_even[blocks + i - base[0] // 2]
        for h in range(2):
            j = 2 * i + h
            odd, even = m_odd[j - base[0]], m_even[j - base[0]]
            for f in range(2):
                came = jnp.where(mine, pick(odd, half + 4 * f), pick(even, half + 4 * f))
                at = (half & 1) + (2 * f + 4 * h)
                force = jnp.where(mine, pick(qs_odd, at), pick(qs_even, at))
                g1[f, j + 1, 0:8] = zero
                g1[f, j + 1, 8:16] = (came + own[f, j]) * keep
                g1[f, j + 1, 16:24] = jnp.where(sub < 4, force, own_q[f, j])

    def second(j):
        jj = j + 1
        mids, nears, fars, forces = [], [], [], []
        for f in range(2):
            mid = g1[f, jj, 8:16]
            near, far = sideways(mid, g1[f, jj - 1, 8:16], g1[f, jj + 1, 8:16], lane)
            turned = turn(mid, 4)
            up = turn(mid, 2)
            nears.append(near + (g1[f, jj, 6:14] + jnp.where(sub < 6, turn(mid, 6), 0.0)))
            fars.append(far + turned)
            forces.append(g1[f, jj, 16:24])
            mids.append(mid)
            g2[f, jj, 8:16] = p2[f, j] + (close[f] * up + wide[f] * turned)
        new = stepped(mids[0], mids[1], nears, fars, forces, 1.0, 0.05)
        for f in range(2):
            g2[f, jj, 0:8] = new[f] * keep

    def third(j):
        cols = block_columns(j)
        jj = j + 1
        mids, nears, fars, forces, deep = [], [], [], [], []
        for f in range(2):
            mid = g2[f, jj, 4:12]
            low2 = g2[f, jj, 8:16]
            near, far = sideways(mid, g2[f, jj - 1, 4:12], g2[f, jj + 1, 4:12], lane)
            nears.append(near + (g2[f, jj, 2:10] + g2[f, jj, 6:14]))
            fars.append(far + (g2[f, jj, 0:8] + low2))
            forces.append(n2[f, j])
            mids.append(mid)
            deep.append(p3[f, j] + (close[f] * turn(low2, 6) + wide[f] * low2))
        new = stepped(mids[0], mids[1], nears, fars, forces, 1.0, 0.05)
        for f in range(2):
            top = jnp.where(sub < 4, pick(new[f], even_rows), pick(deep[f], even_rows))
            low = jnp.where(sub < 4, pick(deep[f], 7 - even_rows), pick(new[f], 7 - even_rows))
            fbuf[f, 0:8, cols] = top
            fbuf[f, 8:16, cols] = low
            cbuf[f, 0:8, cols] = top - spread[j, 2 * f]
            cbuf[f, 8:16, cols] = low - spread[j, 2 * f + 1]

    for f in range(2):
        for edge in (0, nb + 1):
            for r in range(3):
                g1[f, edge, 8 * r : 8 * r + 8] = zero
            for r in range(2):
                g2[f, edge, 8 * r : 8 * r + 8] = zero
    copies = []
    for c, (span1, span2, span3) in enumerate(spans):
        long_loop(span1[0] // 2, span1[1] // 2, first, 16)
        long_loop(*span2, second, MOST)
        long_loop(*span3, third, MOST)
        cols = pl.ds(span3[0] * 128, (span3[1] - span3[0]) * 128)
        for n, (src, dst) in enumerate(((fbuf, fine), (cbuf, corr))):
            copies.append(
                pltpu.make_async_copy(src.at[:, :, cols], dst.at[:, :, cols], sems.at[n, c])
            )
            copies[-1].start()
    for copy in copies:
        copy.wait()


def early_kernel(row_axis, split, *refs):
    ins, outs, carried, scratch = refs[:8], refs[8:10], refs[10:12], refs[12:]
    g1, g2 = scratch[:2]
    mid = split // 2
    spans = [
        ((0, split), (0, split - 1), (0, mid)),
        ((split, split), (split - 1, split - 1), (mid, split - 2)),
    ]
    finish(row_axis, spans, (0, split), *ins, *outs, *scratch)
    for f in range(2):
        for k in range(2):
            for r in range(3):
                carried[0][f, k, 8 * r : 8 * r + 8] = g1[f, split - 1 + k, 8 * r : 8 * r + 8]
            for r in range(2):
                carried[1][f, k, 8 * r : 8 * r + 8] = g2[f, split - 2 + k, 8 * r : 8 * r + 8]


def late_kernel(row_axis, split, *refs):
    ins, carried, outs, scratch = refs[:8], refs[8:10], refs[12:14], refs[14:]
    g1, g2 = scratch[:2]
    nb = ins[2].shape[1]
    for f in range(2):
        for k in range(2):
            for r in range(3):
                g1[f, split - 1 + k, 8 * r : 8 * r + 8] = carried[0][f, k, 8 * r : 8 * r + 8]
            for r in range(2):
                g2[f, split - 2 + k, 8 * r : 8 * r + 8] = carried[1][f, k, 8 * r : 8 * r + 8]
    mid = split + (nb - split) // 2
    spans = [
        ((split, nb), (split - 1, nb), (split - 2, mid)),
        ((nb, nb), (nb, nb), (mid, nb)),
    ]
    finish(row_axis, spans, (split, nb), *ins, *outs, *scratch)


def in_vmem(x):
    return pltpu.with_memory_space_constraint(x, pltpu.VMEM)


def in_hbm(x):
    return pltpu.with_memory_space_constraint(x, pltpu.HBM)


def spec(space):
    return pl.BlockSpec(memory_space=space)


def call(kernel, name, mib, ins, outs, scratch, hbm_ins=(), hbm_outs=(), aliases=None):
    return pl.pallas_call(
        kernel,
        out_shape=tuple(hbm_outs) + tuple(outs),
        in_specs=[spec(pltpu.VMEM)] * len(ins) + [spec(pltpu.HBM)] * len(hbm_ins),
        out_specs=(spec(pltpu.HBM),) * len(hbm_outs) + (spec(pltpu.VMEM),) * len(outs),
        scratch_shapes=scratch,
        input_output_aliases=aliases or {},
        compiler_params=pltpu.CompilerParams(vmem_limit_bytes=mib * MIB),
        name=name,
    )(*(in_vmem(x) for x in ins), *(in_hbm(x) for x in hbm_ins))


def shards(count, fine_state, noise):
    f32 = jnp.float32
    wide = fine_state.shape[2]
    nb = wide // 128
    groups = nb // 4
    split = nb // 2 + 8

    def vmem(*shape):
        return pltpu.VMEM(shape, f32)

    pairs = [(i, i + 1) for i in range(1, count - 1, 2)]
    odd = pairs + [(b, a) for a, b in pairs]
    pairs = [(i, i + 1) for i in range(0, count - 1, 2)]
    even = pairs + [(b, a) for a, b in pairs]

    a_rows = split + split // 2 + groups // 2
    a_odd, a_even, x0, f1, own, own_q, start, held_noise = call(
        functools.partial(start_kernel, "row", split),
        "start",
        16,
        [],
        [
            vmem(a_rows, 8, 128),
            vmem(a_rows, 8, 128),
            vmem(2, nb + 2, 24, 128),
            vmem(2, nb + 2, 8, 128),
            vmem(2, nb, 8, 128),
            vmem(2, nb, 8, 128),
            vmem(groups + 2, 8, 128),
            pltpu.VMEM(noise.shape, noise.dtype),
        ],
        [vmem(2, 16, wide), vmem(4, groups, 8, 128), pltpu.SemaphoreType.DMA((CHUNKS + 3,))],
        hbm_ins=[fine_state, noise],
    )
    a_odd = lax.ppermute(a_odd, "row", odd)
    a_even = lax.ppermute(a_even, "row", even)

    b_rows = (nb - split) + (nb - split) // 2
    b_odd, b_even, f1, own, own_q = call(
        functools.partial(edge_kernel, "row", split),
        "edge",
        16,
        [x0, held_noise, f1, own, own_q],
        [
            vmem(b_rows, 8, 128),
            vmem(b_rows, 8, 128),
            vmem(2, nb + 2, 8, 128),
            vmem(2, nb, 8, 128),
            vmem(2, nb, 8, 128),
        ],
        [],
        aliases={2: 2, 3: 3, 4: 4},
    )
    b_odd = lax.ppermute(b_odd, "row", odd)
    b_even = lax.ppermute(b_even, "row", even)

    p2, p3, n2, part = call(
        inner_kernel,
        "inner",
        16,
        [x0, f1, held_noise, start],
        [vmem(2, nb, 8, 128)] * 3 + [vmem(groups, 8, 128)],
        [vmem(2, nb + 2, 8, 128)] * 2 + [vmem(4, groups, 8, 128)],
    )
    coarse, spread = call(
        functools.partial(coarse_kernel, "row"),
        "coarse",
        16,
        [part, a_odd, a_even],
        [jax.ShapeDtypeStruct((2, 4, groups * 128), f32), vmem(nb, 4, 8, 128)],
        [vmem(4, groups, 8, 128), vmem(groups, 8, 128)],
    )
    work = [
        vmem(2, nb + 2, 24, 128),
        vmem(2, nb + 2, 16, 128),
        vmem(2, 16, wide),
        vmem(2, 16, wide),
        pltpu.SemaphoreType.DMA((2, 2)),
    ]
    whole = [jax.ShapeDtypeStruct((2, 16, wide), f32)] * 2
    fine, corr, last1, last2 = call(
        functools.partial(early_kernel, "row", split),
        "early",
        16,
        [a_odd, a_even, own, own_q, p2, p3, n2, spread],
        [vmem(2, 2, 24, 128), vmem(2, 2, 16, 128)],
        work,
        hbm_outs=whole,
    )
    fine, corr = call(
        functools.partial(late_kernel, "row", split),
        "late",
        16,
        [b_odd, b_even, own, own_q, p2, p3, n2, spread, last1, last2],
        [],
        work,
        hbm_ins=[fine, corr],
        hbm_outs=whole,
        aliases={10: 0, 11: 1},
    )
    return fine, coarse, corr


def solution(mesh):
    rows = P("sample", "row", None)
    return jax.shard_map(
        functools.partial(shards, mesh.shape["row"]),
        mesh=mesh,
        in_specs=(rows, P("sample", None, "row", None)),
        out_specs=(rows, rows, rows),
        check_vma=False,
    )
```

```python
import functools

import jax
import jax.numpy as jnp
from jax import lax
from jax.experimental import pallas as pl
from jax.experimental.pallas import tpu as pltpu
from jax.sharding import PartitionSpec as P

NEAR, FAR = 4.0 / 3.0, -1.0 / 12.0
DIFFUSE = (0.15, 0.05)
MIB = 1 << 20
CHUNKS = 8
MOST = 48


def iota(dim):
    return lax.broadcasted_iota(jnp.int32, (8, 128), dim)


def pick(x, index):
    return jnp.take_along_axis(x, index, axis=0, mode="promise_in_bounds")


def turn(x, steps):
    return pltpu.roll(x, steps, 0)


def sideways(mid, left, right, lane):
    near = pltpu.roll(jnp.where(lane == 127, left, mid), 1, 1) + pltpu.roll(
        jnp.where(lane == 0, right, mid), 127, 1
    )
    far = pltpu.roll(jnp.where(lane >= 126, left, mid), 2, 1) + pltpu.roll(
        jnp.where(lane < 2, right, mid), 126, 1
    )
    return near, far


def stepped(a, b, near, far, force, scale, react):
    da, db = DIFFUSE[0] * scale, DIFFUSE[1] * scale
    new_a = a * ((1.0 + react - 5.0 * da) - (react / 3.0) * (a * a)) - react * b
    new_a = new_a + (da * NEAR) * near[0] + (da * FAR) * far[0] + force[0]
    low = 0.08 * react
    new_b = b * (1.0 - 5.0 * db - 0.8 * low) + low * a + 0.7 * low
    new_b = new_b + (db * NEAR) * near[1] + (db * FAR) * far[1] + force[1]
    return new_a, new_b


def both_ends(block, first, sub):
    block = block.astype(jnp.float32)
    half = sub >> 1
    top = pick(block[0:8], half + first)
    low = pick(block[8:16], 7 - first - half)
    return jnp.where((sub & 1) == 0, top, low)


def loop(lo, hi, body, unroll):
    if hi > lo:
        lax.fori_loop(lo, hi, lambda i, c: (body(i), c)[1], 0, unroll=unroll)


def long_loop(lo, hi, body, most):
    if hi <= lo:
        return
    steps = -(-(hi - lo) // most)
    each = (hi - lo) // steps
    last = lo + (steps - 1) * each
    loop(lo, last, body, each)
    for j in range(last, hi):
        body(j)


def block_columns(j):
    return pl.ds(pl.multiple_of(j * 128, 128), 128)


def selection(k, value, transpose):
    shape = (256, 128)
    row = lax.broadcasted_iota(jnp.int32, shape, 0) & 127
    col = lax.broadcasted_iota(jnp.int32, shape, 1)
    fine, coarse = (col, row) if transpose else (row, col)
    return jnp.where(coarse == 32 * k + (fine >> 2), value, 0.0).astype(jnp.bfloat16)


def in_two(x):
    high = x.astype(jnp.bfloat16)
    low = (x - high.astype(jnp.float32)).astype(jnp.bfloat16)
    return jnp.concatenate([high, low], axis=1)


def lanes_averaged(held):
    groups = held.shape[1]
    total = jnp.zeros((groups * 8, 128), jnp.float32)
    for k in range(4):
        total = total + jnp.dot(
            in_two(held[k].reshape(groups * 8, 128)),
            selection(k, 1.0 / 16.0, False),
            preferred_element_type=jnp.float32,
        )
    return total.reshape(groups, 8, 128)


def edge_rows(parity, split, x0, noise, m_odd, m_even, f1, own, own_q):
    sub, lane = iota(0), iota(1)
    strong = [jnp.where((sub & 6) == 2, DIFFUSE[f] * NEAR, 0.0) for f in range(2)]
    wins_at = [6 - 2 * (sub & 3) + side for side in (parity, 1 - parity)]
    qs_at = [2 - 2 * (sub & 1) + side for side in (parity, 1 - parity)]

    def step(j):
        cols = block_columns(j)
        jj = j + 1
        mids, nears, fars, forces, rims = [], [], [], [], []
        for f in range(2):
            mid, up1 = x0[f, jj, 8:16], x0[f, jj, 6:14]
            near, far = sideways(mid, x0[f, jj - 1, 8:16], x0[f, jj + 1, 8:16], lane)
            nears.append(near + (up1 + x0[f, jj, 10:18]))
            fars.append(far + (x0[f, jj, 4:12] + x0[f, jj, 12:20]))
            forces.append(0.25 * both_ends(noise[0, f, :, cols], 0, sub))
            mids.append(mid)
            rims.append((DIFFUSE[f] * NEAR) * up1 + (DIFFUSE[f] * FAR) * mid)
        new = stepped(mids[0], mids[1], nears, fars, forces, 1.0, 0.05)
        wins, qs = [], []
        for f in range(2):
            half = turn(new[f], 4)
            f1[f, jj] = new[f]
            win = jnp.where(sub < 4, rims[f], half)
            own[f, j] = win
            q = 0.25 * both_ends(noise[1, f, :, cols], 0, sub)
            q = q + (DIFFUSE[f] * FAR) * half + strong[f] * turn(new[f], 6)
            own_q[f, j] = turn(q, 4)
            wins.append(win)
            qs.append(q)
        return wins, qs

    def pair(i):
        wins0, qs0 = step(2 * i)
        wins1, qs1 = step(2 * i + 1)
        base = split[0]
        blocks = split[1] - split[0]
        for n, out in enumerate((m_odd, m_even)):
            at = wins_at[n]
            k = 2 * i - base
            out[k] = jnp.where(sub < 4, pick(wins0[0], at), pick(wins0[1], at))
            out[k + 1] = jnp.where(sub < 4, pick(wins1[0], at), pick(wins1[1], at))
            at = qs_at[n]
            first = jnp.where((sub & 2) == 0, pick(qs0[0], at), pick(qs0[1], at))
            second = jnp.where((sub & 2) == 0, pick(qs1[0], at), pick(qs1[1], at))
            out[blocks + i - base // 2] = jnp.where(sub < 4, first, second)

    long_loop(split[0] // 2, split[1] // 2, pair, 18)


def start_kernel(
    row_axis, split, f_hbm, n_hbm, m_odd, m_even, x0, f1, own, own_q, start, noise, fbuf, held, sems
):
    nb = x0.shape[1] - 2
    groups = nb // 4
    width = nb // CHUNKS
    first, rest = [], []
    for c in range(CHUNKS):
        cols = pl.ds(c * width * 128, width * 128)
        first.append(pltpu.make_async_copy(f_hbm.at[:, :, cols], fbuf.at[:, :, cols], sems.at[c]))
    sooner, later = pl.ds(0, split * 128), pl.ds(split * 128, (nb - split) * 128)
    early = pltpu.make_async_copy(
        n_hbm.at[0:2, :, :, sooner], noise.at[0:2, :, :, sooner], sems.at[CHUNKS]
    )
    rest.append(
        pltpu.make_async_copy(
            n_hbm.at[0:2, :, :, later], noise.at[0:2, :, :, later], sems.at[CHUNKS + 1]
        )
    )
    rest.append(pltpu.make_async_copy(n_hbm.at[2:3], noise.at[2:3], sems.at[CHUNKS + 2]))
    for copy in first + [early] + rest:
        copy.start()
    sub = iota(0)
    half = sub >> 1
    parity = lax.rem(lax.axis_index(row_axis), 2)
    zero = jnp.zeros((8, 128), jnp.float32)
    for f in range(2):
        for edge in (0, nb + 1):
            for r in range(3):
                x0[f, edge, 8 * r : 8 * r + 8] = zero
            f1[f, edge] = zero
    start[0] = zero
    start[groups + 1] = zero

    def block(j):
        cols = block_columns(j)
        sums = []
        for f in range(2):
            top, low = fbuf[f, 0:8, cols], fbuf[f, 8:16, cols]
            outer = jnp.where((sub & 1) == 0, pick(top, half), pick(low, 7 - half))
            inner = jnp.where((sub & 1) == 0, pick(top, half + 4), pick(low, 3 - half))
            x0[f, j + 1, 0:8] = zero
            x0[f, j + 1, 8:16] = outer
            x0[f, j + 1, 16:24] = inner
            parts = []
            for x in (outer, inner):
                x = x + turn(x, 4)
                parts.append(x + turn(x, 2))
            sums.append(jnp.where((sub & 3) < 2, parts[0], parts[1]))
        return jnp.where(sub < 4, sums[0], sums[1])

    def group(g):
        for k in range(4):
            held[k, g] = block(4 * g + k)

    for c in range(CHUNKS):
        first[c].wait()
        loop(c * width // 4, (c + 1) * width // 4, group, 4)
    start[1 : groups + 1] = lanes_averaged(held)
    offset = m_odd.shape[0] - groups // 2

    def message(i):
        rims = []
        for h in range(2):
            c = start[2 * i + h + 1]
            rims.append(jnp.where((sub & 2) == 0, NEAR * c, 0.0) + FAR * pick(c, sub ^ 2))
        for out, side in ((m_odd, parity), (m_even, 1 - parity)):
            at = (2 * sub + side) & 7
            out[offset + i] = jnp.where(sub < 4, pick(rims[0], at), pick(rims[1], at))

    loop(0, groups // 2, message, 8)
    early.wait()
    edge_rows(parity, (0, split), x0, noise, m_odd, m_even, f1, own, own_q)
    for copy in rest:
        copy.wait()


def edge_kernel(row_axis, split, x0, noise, f1_in, own_in, q_in, m_odd, m_even, f1, own, own_q):
    del f1_in, own_in, q_in
    parity = lax.rem(lax.axis_index(row_axis), 2)
    edge_rows(parity, (split, own.shape[1]), x0, noise, m_odd, m_even, f1, own, own_q)


def inner_kernel(x0, f1, noise, start, p2, p3, n2, part, g1, g2, held):
    nb = x0.shape[1] - 2
    sub, lane = iota(0), iota(1)
    zero = jnp.zeros((8, 128), jnp.float32)
    for f in range(2):
        for edge in (0, nb + 1):
            g1[f, edge] = zero
            g2[f, edge] = zero
    down1 = jnp.where(sub < 6, sub + 2, 13 - sub)
    down2 = jnp.where(sub < 4, sub + 4, 11 - sub)

    def first(j):
        cols = block_columns(j)
        jj = j + 1
        mids, nears, fars, forces = [], [], [], []
        for f in range(2):
            mid = x0[f, jj, 16:24]
            near, far = sideways(mid, x0[f, jj - 1, 16:24], x0[f, jj + 1, 16:24], lane)
            nears.append(near + (x0[f, jj, 14:22] + pick(mid, down1)))
            fars.append(far + (x0[f, jj, 12:20] + pick(mid, down2)))
            forces.append(0.25 * both_ends(noise[0, f, :, cols], 4, sub))
            mids.append(mid)
        new = stepped(mids[0], mids[1], nears, fars, forces, 1.0, 0.05)
        for f in range(2):
            g1[f, jj] = new[f]

    def second(j):
        cols = block_columns(j)
        jj = j + 1
        mids, nears, fars, forces = [], [], [], []
        tops, top_nears, top_fars, top_forces = [], [], [], []
        for f in range(2):
            mid, top = g1[f, jj], f1[f, jj]
            top2, mid2, top4, mid4 = turn(top, 2), turn(mid, 2), turn(top, 4), turn(mid, 4)
            low2 = jnp.where(sub < 4, top4, mid4)
            near, far = sideways(mid, g1[f, jj - 1], g1[f, jj + 1], lane)
            nears.append(near + (jnp.where(sub < 2, top2, mid2) + pick(mid, down1)))
            fars.append(far + (low2 + pick(mid, down2)))
            noises = noise[1, f, :, cols]
            forces.append(0.25 * both_ends(noises, 4, sub))
            mids.append(mid)
            near, far = sideways(top, f1[f, jj - 1], f1[f, jj + 1], lane)
            up1 = jnp.where(sub < 6, 0.0, top2)
            low1 = jnp.where(sub < 6, turn(top, 6), turn(mid, 6))
            top_nears.append(near + (up1 + low1))
            top_fars.append(far + low2)
            top_forces.append(0.25 * both_ends(noises, 0, sub))
            tops.append(top)
        new = stepped(mids[0], mids[1], nears, fars, forces, 1.0, 0.05)
        part = stepped(tops[0], tops[1], top_nears, top_fars, top_forces, 1.0, 0.05)
        for f in range(2):
            g2[f, jj] = new[f]
            p2[f, j] = jnp.where(sub < 4, turn(part[f], 4), turn(new[f], 4))

    def third(j):
        cols = block_columns(j)
        jj = j + 1
        mids, nears, fars, forces = [], [], [], []
        for f in range(2):
            mid = g2[f, jj]
            near, far = sideways(mid, g2[f, jj - 1], g2[f, jj + 1], lane)
            up1 = jnp.where(sub < 2, 0.0, turn(mid, 2))
            up2 = jnp.where(sub < 4, 0.0, turn(mid, 4))
            nears.append(near + (up1 + pick(mid, down1)))
            fars.append(far + (up2 + pick(mid, down2)))
            noises = noise[2, f, :, cols]
            forces.append(0.25 * both_ends(noises, 4, sub))
            n2[f, j] = 0.25 * both_ends(noises, 0, sub)
            mids.append(mid)
        new = stepped(mids[0], mids[1], nears, fars, forces, 1.0, 0.05)
        for f in range(2):
            p3[f, j] = new[f]

    loop(0, nb, first, 32)
    loop(0, nb, second, 32)
    loop(0, nb, third, 32)
    coarse_alone(start, noise, part, held)


def coarse_alone(start, noise, part, held):
    groups = part.shape[0]
    sub, lane = iota(0), iota(1)

    def gather_noise(g):
        for k in range(4):
            cols = block_columns(4 * g + k)
            sums = []
            for f in range(2):
                total = noise[0, f, :, cols].astype(jnp.float32)
                total = total + noise[1, f, :, cols].astype(jnp.float32)
                total = total + noise[2, f, :, cols].astype(jnp.float32)
                parts = []
                for r in (0, 8):
                    x = total[r : r + 8]
                    x = x + turn(x, 7)
                    parts.append(x + turn(x, 6))
                sums.append(
                    jnp.where(
                        (sub & 1) == 0,
                        pick(parts[0], (sub & 2) * 2),
                        pick(parts[1], 4 - (sub & 2) * 2),
                    )
                )
            held[k, g] = jnp.where(sub < 4, sums[0], sums[1])

    loop(0, groups, gather_noise, 4)
    part[...] = lanes_averaged(held)

    is_a = sub < 4
    scale, react = 3.0 / 16.0, 0.15
    diffuse = jnp.where(is_a, DIFFUSE[0] * scale, DIFFUSE[1] * scale)
    inward = jnp.where((sub & 2) == 0, sub + 2, sub ^ 1)

    def update(g):
        c = start[g + 1]
        near, far = sideways(c, start[g], start[g + 2], lane)
        near = near + pick(c, inward) + jnp.where((sub & 2) == 0, 0.0, turn(c, 2))
        far = far + pick(c, (sub & 4) + 3 - (sub & 3))
        lap = NEAR * near + FAR * far - 5.0 * c
        other = turn(c, 4)
        change = jnp.where(
            is_a,
            react * (c - c * c * c / 3.0 - other),
            (react * 0.08) * (other + 0.7 - 0.8 * c),
        )
        part[g] = c + diffuse * lap + change + part[g]

    loop(0, groups, update, 16)


def coarse_kernel(row_axis, part, a_odd, a_even, coarse, spread, held, new):
    groups = part.shape[0]
    offset = a_odd.shape[0] - groups // 2
    sub = iota(0)
    parity = lax.rem(lax.axis_index(row_axis), 2)
    mine = (sub & 1) == parity
    scale = 3.0 / 16.0
    diffuse = jnp.where(sub < 4, DIFFUSE[0] * scale, DIFFUSE[1] * scale)
    order = jnp.where(sub < 1, 0, jnp.where(sub < 2, 2, jnp.where(sub < 3, 3, 1)))

    def add_rim(i):
        odd, even = a_odd[offset + i], a_even[offset + i]
        for h in range(2):
            g = 2 * i + h
            at = 4 * h + (sub >> 1)
            rim = jnp.where(mine, pick(odd, at), pick(even, at))
            whole = part[g] + diffuse * rim
            new[g] = whole
            cols = block_columns(g)
            for f in range(2):
                coarse[f, :, cols] = pick(whole, order + 4 * f)[0:4]

    loop(0, groups // 2, add_rim, 8)
    whole = in_two(new[...].reshape(groups * 8, 128))
    for k in range(4):
        held[k] = jnp.dot(
            whole, selection(k, 1.0, True), preferred_element_type=jnp.float32
        ).reshape(groups, 8, 128)

    def spread_rows(g):
        for k in range(4):
            x = held[k, g]
            for f in range(2):
                spread[4 * g + k, 2 * f] = pick(x, 4 * f + jnp.where(sub < 4, 0, 2))
                spread[4 * g + k, 2 * f + 1] = pick(x, 4 * f + jnp.where(sub < 4, 3, 1))

    loop(0, groups, spread_rows, 8)


def finish(
    row_axis, spans, base, m_odd, m_even, own, own_q, p2, p3, n2, spread, fine, corr, g1, g2, fbuf, cbuf, sems
):
    nb = own.shape[1]
    blocks = base[1] - base[0]
    sub, lane = iota(0), iota(1)
    place = lax.axis_index(row_axis)
    parity = lax.rem(place, 2)
    last = lax.axis_size(row_axis) - 1
    mine = (sub & 1) == parity
    outside = ((place == 0) & ((sub & 1) == 0)) | ((place == last) & ((sub & 1) == 1))
    keep = jnp.where(outside & (sub < 4), jnp.float32(0.0), jnp.float32(1.0))
    half = sub >> 1
    zero = jnp.zeros((8, 128), jnp.float32)
    close = [jnp.where(sub < 2, DIFFUSE[f] * NEAR, 0.0) for f in range(2)]
    wide = [jnp.where(sub < 4, DIFFUSE[f] * FAR, 0.0) for f in range(2)]
    even_rows = (2 * sub) & 7

    def first(i):
        qs_odd = m_odd[blocks + i - base[0] // 2]
        qs_even = m_even[blocks + i - base[0] // 2]
        for h in range(2):
            j = 2 * i + h
            odd, even = m_odd[j - base[0]], m_even[j - base[0]]
            for f in range(2):
                came = jnp.where(mine, pick(odd, half + 4 * f), pick(even, half + 4 * f))
                at = (half & 1) + (2 * f + 4 * h)
                force = jnp.where(mine, pick(qs_odd, at), pick(qs_even, at))
                g1[f, j + 1, 8:16] = (came + own[f, j]) * keep
                g1[f, j + 1, 16:24] = jnp.where(sub < 4, force, own_q[f, j])

    def second(j):
        jj = j + 1
        mids, nears, fars, forces = [], [], [], []
        for f in range(2):
            mid = g1[f, jj, 8:16]
            near, far = sideways(mid, g1[f, jj - 1, 8:16], g1[f, jj + 1, 8:16], lane)
            turned = turn(mid, 4)
            up = turn(mid, 2)
            up1 = jnp.where(sub < 2, 0.0, up)
            nears.append(near + (up1 + jnp.where(sub < 6, turn(mid, 6), 0.0)))
            fars.append(far + turned)
            forces.append(g1[f, jj, 16:24])
            mids.append(mid)
            g2[f, jj, 8:16] = p2[f, j] + (close[f] * up + wide[f] * turned)
        new = stepped(mids[0], mids[1], nears, fars, forces, 1.0, 0.05)
        for f in range(2):
            g2[f, jj, 0:8] = new[f] * keep

    def third(j):
        cols = block_columns(j)
        jj = j + 1
        mids, nears, fars, forces, deep = [], [], [], [], []
        for f in range(2):
            mid = g2[f, jj, 4:12]
            low2 = g2[f, jj, 8:16]
            near, far = sideways(mid, g2[f, jj - 1, 4:12], g2[f, jj + 1, 4:12], lane)
            nears.append(near + (g2[f, jj, 2:10] + g2[f, jj, 6:14]))
            fars.append(far + (g2[f, jj, 0:8] + low2))
            forces.append(n2[f, j])
            mids.append(mid)
            deep.append(p3[f, j] + (close[f] * turn(low2, 6) + wide[f] * low2))
        new = stepped(mids[0], mids[1], nears, fars, forces, 1.0, 0.05)
        for f in range(2):
            top = jnp.where(sub < 4, pick(new[f], even_rows), pick(deep[f], even_rows))
            low = jnp.where(sub < 4, pick(deep[f], 7 - even_rows), pick(new[f], 7 - even_rows))
            fbuf[f, 0:8, cols] = top
            fbuf[f, 8:16, cols] = low
            cbuf[f, 0:8, cols] = top - spread[j, 2 * f]
            cbuf[f, 8:16, cols] = low - spread[j, 2 * f + 1]

    for f in range(2):
        for edge in (0, nb + 1):
            for r in range(3):
                g1[f, edge, 8 * r : 8 * r + 8] = zero
            for r in range(2):
                g2[f, edge, 8 * r : 8 * r + 8] = zero
    copies = []
    for c, (span1, span2, span3) in enumerate(spans):
        long_loop(span1[0] // 2, span1[1] // 2, first, 16)
        long_loop(*span2, second, MOST)
        long_loop(*span3, third, MOST)
        cols = pl.ds(span3[0] * 128, (span3[1] - span3[0]) * 128)
        for n, (src, dst) in enumerate(((fbuf, fine), (cbuf, corr))):
            copies.append(
                pltpu.make_async_copy(src.at[:, :, cols], dst.at[:, :, cols], sems.at[n, c])
            )
            copies[-1].start()
    for copy in copies:
        copy.wait()


def early_kernel(row_axis, split, *refs):
    ins, outs, carried, scratch = refs[:8], refs[8:10], refs[10:12], refs[12:]
    g1, g2 = scratch[:2]
    mid = split // 2
    spans = [
        ((0, split), (0, split - 1), (0, mid)),
        ((split, split), (split - 1, split - 1), (mid, split - 2)),
    ]
    finish(row_axis, spans, (0, split), *ins, *outs, *scratch)
    for f in range(2):
        for k in range(2):
            for r in range(3):
                carried[0][f, k, 8 * r : 8 * r + 8] = g1[f, split - 1 + k, 8 * r : 8 * r + 8]
            for r in range(2):
                carried[1][f, k, 8 * r : 8 * r + 8] = g2[f, split - 2 + k, 8 * r : 8 * r + 8]


def late_kernel(row_axis, split, *refs):
    ins, carried, outs, scratch = refs[:8], refs[8:10], refs[12:14], refs[14:]
    g1, g2 = scratch[:2]
    nb = ins[2].shape[1]
    for f in range(2):
        for k in range(2):
            for r in range(3):
                g1[f, split - 1 + k, 8 * r : 8 * r + 8] = carried[0][f, k, 8 * r : 8 * r + 8]
            for r in range(2):
                g2[f, split - 2 + k, 8 * r : 8 * r + 8] = carried[1][f, k, 8 * r : 8 * r + 8]
    mid = split + (nb - split) // 2
    spans = [
        ((split, nb), (split - 1, nb), (split - 2, mid)),
        ((nb, nb), (nb, nb), (mid, nb)),
    ]
    finish(row_axis, spans, (split, nb), *ins, *outs, *scratch)


def in_vmem(x):
    return pltpu.with_memory_space_constraint(x, pltpu.VMEM)


def in_hbm(x):
    return pltpu.with_memory_space_constraint(x, pltpu.HBM)


def spec(space):
    return pl.BlockSpec(memory_space=space)


def call(kernel, name, mib, ins, outs, scratch, hbm_ins=(), hbm_outs=(), aliases=None):
    return pl.pallas_call(
        kernel,
        out_shape=tuple(hbm_outs) + tuple(outs),
        in_specs=[spec(pltpu.VMEM)] * len(ins) + [spec(pltpu.HBM)] * len(hbm_ins),
        out_specs=(spec(pltpu.HBM),) * len(hbm_outs) + (spec(pltpu.VMEM),) * len(outs),
        scratch_shapes=scratch,
        input_output_aliases=aliases or {},
        compiler_params=pltpu.CompilerParams(vmem_limit_bytes=mib * MIB),
        name=name,
    )(*(in_vmem(x) for x in ins), *(in_hbm(x) for x in hbm_ins))


def shards(count, fine_state, noise):
    f32 = jnp.float32
    wide = fine_state.shape[2]
    nb = wide // 128
    groups = nb // 4
    split = nb // 2 + 8

    def vmem(*shape):
        return pltpu.VMEM(shape, f32)

    pairs = [(i, i + 1) for i in range(1, count - 1, 2)]
    odd = pairs + [(b, a) for a, b in pairs]
    pairs = [(i, i + 1) for i in range(0, count - 1, 2)]
    even = pairs + [(b, a) for a, b in pairs]

    a_rows = split + split // 2 + groups // 2
    a_odd, a_even, x0, f1, own, own_q, start, held_noise = call(
        functools.partial(start_kernel, "row", split),
        "start",
        16,
        [],
        [
            vmem(a_rows, 8, 128),
            vmem(a_rows, 8, 128),
            vmem(2, nb + 2, 24, 128),
            vmem(2, nb + 2, 8, 128),
            vmem(2, nb, 8, 128),
            vmem(2, nb, 8, 128),
            vmem(groups + 2, 8, 128),
            pltpu.VMEM(noise.shape, noise.dtype),
        ],
        [vmem(2, 16, wide), vmem(4, groups, 8, 128), pltpu.SemaphoreType.DMA((CHUNKS + 3,))],
        hbm_ins=[fine_state, noise],
    )
    a_odd = lax.ppermute(a_odd, "row", odd)
    a_even = lax.ppermute(a_even, "row", even)

    b_rows = (nb - split) + (nb - split) // 2
    b_odd, b_even, f1, own, own_q = call(
        functools.partial(edge_kernel, "row", split),
        "edge",
        16,
        [x0, held_noise, f1, own, own_q],
        [
            vmem(b_rows, 8, 128),
            vmem(b_rows, 8, 128),
            vmem(2, nb + 2, 8, 128),
            vmem(2, nb, 8, 128),
            vmem(2, nb, 8, 128),
        ],
        [],
        aliases={2: 2, 3: 3, 4: 4},
    )
    b_odd = lax.ppermute(b_odd, "row", odd)
    b_even = lax.ppermute(b_even, "row", even)

    p2, p3, n2, part = call(
        inner_kernel,
        "inner",
        16,
        [x0, f1, held_noise, start],
        [vmem(2, nb, 8, 128)] * 3 + [vmem(groups, 8, 128)],
        [vmem(2, nb + 2, 8, 128)] * 2 + [vmem(4, groups, 8, 128)],
    )
    coarse, spread = call(
        functools.partial(coarse_kernel, "row"),
        "coarse",
        16,
        [part, a_odd, a_even],
        [jax.ShapeDtypeStruct((2, 4, groups * 128), f32), vmem(nb, 4, 8, 128)],
        [vmem(4, groups, 8, 128), vmem(groups, 8, 128)],
    )
    work = [
        vmem(2, nb + 2, 24, 128),
        vmem(2, nb + 2, 16, 128),
        vmem(2, 16, wide),
        vmem(2, 16, wide),
        pltpu.SemaphoreType.DMA((2, 2)),
    ]
    whole = [jax.ShapeDtypeStruct((2, 16, wide), f32)] * 2
    fine, corr, last1, last2 = call(
        functools.partial(early_kernel, "row", split),
        "early",
        16,
        [a_odd, a_even, own, own_q, p2, p3, n2, spread],
        [vmem(2, 2, 24, 128), vmem(2, 2, 16, 128)],
        work,
        hbm_outs=whole,
    )
    fine, corr = call(
        functools.partial(late_kernel, "row", split),
        "late",
        16,
        [b_odd, b_even, own, own_q, p2, p3, n2, spread, last1, last2],
        [],
        work,
        hbm_ins=[fine, corr],
        hbm_outs=whole,
        aliases={10: 0, 11: 1},
    )
    return fine, coarse, corr


def solution(mesh):
    rows = P("sample", "row", None)
    return jax.shard_map(
        functools.partial(shards, mesh.shape["row"]),
        mesh=mesh,
        in_specs=(rows, P("sample", None, "row", None)),
        out_specs=(rows, rows, rows),
        check_vma=False,
    )
```
